32 devices in a mesh: sec: 4 (over y, core), proto: 8 (over z, x).
Axes of the slice: x: 2, y: 2, z: 4, core: 2. Of those that a mesh axis runs over, the one named last changes fastest.
Arguments:
- features: bfloat16 [2048, 512], P('sec'), may hold values from -700 to 700
- prototypes: bfloat16 [512, 262144], P(None, 'proto'), may hold values from -20 to 20
- crop_sample: int32 [2048], P('sec'), may hold values from 0 to 511, as said below
- crop_live: int32 [2048], P('sec'), may hold values 0 or 1
Outputs:
- crop_loss: float32 [2048], P('sec')
- embed_grad: float32 [2048, 512], P(('sec', 'proto'))
The draws below stay inside these ranges and needn't reach their ends.
Inputs may be any that keep to these rules, and one draw needn't show every extreme that they name: `crop_sample`: on student rows the index of a teacher row, 0 to 511; the entries on teacher rows are not read.
All inputs are finite; a program needn't handle non-finite values. No bound on the sum of `crop_live` on one device may be relied on, other than what follows from the above.
Results may differ from the reference program's by a relative error of at most 0.0067.
Values may be sent and summed in bfloat16 or wider, within the bound.
A program may use at most 448 MiB of HBM per device.

```python
import math
import jax
import jax.numpy as jnp
from jax import lax

WIDTH = 512
PROTOS = 262144
ROWS_DEV = 512
ITERS = 3
SAMPLES = 512
TEACH_FIRST = 1024
ALL_ROWS = 2048


def draw_features(key, part):
    keys = jax.random.split(jax.random.fold_in(key, 11), 3)
    drawn = jnp.clip(jax.random.normal(keys[0], (ALL_ROWS, WIDTH), jnp.float32), -6.0, 6.0)
    row_scale = jnp.exp(jax.random.uniform(keys[1], (ALL_ROWS, 1), jnp.float32, 0.0, math.log(10.0)))
    col_factor = jnp.exp(jax.random.uniform(keys[2], (1, WIDTH), jnp.float32, 0.0, math.log(10.0)))
    values = drawn * col_factor * row_scale
    return values.astype(jnp.bfloat16)


def draw_prototypes(key, part):
    noise_key = jax.random.fold_in(key, 13)
    values = jnp.clip(0.3 * jax.random.normal(noise_key, (WIDTH, PROTOS), jnp.float32), -1.8, 1.8)
    return values.astype(jnp.bfloat16)


def draw_crop_sample(key, part):
    picks = jax.random.randint(jax.random.fold_in(key, 17), (ALL_ROWS,), 0, SAMPLES, jnp.int32)
    return picks.at[0].set(SAMPLES - 1).at[1].set(0)


def set_ends(array, key, smallest, top_value):
    longest = array.shape.index(max(array.shape))
    spots = []
    for shift in (0, 1):
        where = [jax.random.randint(jax.random.fold_in(key, axis), (), 0, length) for axis, length in enumerate(array.shape)]
        where[longest] = (where[longest] + shift) % array.shape[longest]
        spots.append(tuple(where))
    return array.at[spots[0]].set(smallest).at[spots[1]].set(top_value)


def setup_inputs(seed: int = 0) -> dict:
    splits = jax.random.split(jax.random.key(seed), 5)
    features = draw_features(jax.random.fold_in(splits[4], 71), 0)
    prototypes = draw_prototypes(jax.random.fold_in(splits[4], 71), 0)
    crop_sample = draw_crop_sample(jax.random.fold_in(splits[4], 71), 0)
    crop_live = set_ends((jax.random.randint(splits[3], (ALL_ROWS,), 0, 4) < 3).astype(jnp.int32), jax.random.fold_in(splits[3], 1), 0, 1)
    return dict(features=features, prototypes=prototypes, crop_sample=crop_sample, crop_live=crop_live)


TEACH_TEMP = 0.07
STUD_TEMP = 0.1

def unit_rows_of(features):
    values = features.astype(jnp.float32)
    scaled = values * lax.rsqrt(lax.optimization_barrier(jnp.sum(values * values, axis=1, keepdims=True)) + 1e-06)
    return scaled.astype(jnp.bfloat16)

def reference(features, prototypes, crop_sample, crop_live):
    unit_rows = unit_rows_of(features)
    teach_end = TEACH_FIRST + SAMPLES
    teacher_logits = jnp.dot(unit_rows[TEACH_FIRST:teach_end], prototypes, preferred_element_type=jnp.float32) / TEACH_TEMP
    row_top = lax.optimization_barrier(jnp.max(teacher_logits, axis=1, keepdims=True))
    expo_tab = jnp.exp(teacher_logits - row_top)
    row_weight = jnp.ones((SAMPLES,), jnp.float32)
    col_scale = jnp.ones((PROTOS,), jnp.float32)
    for sweep in range(ITERS):
        col_scale = 1.0 / (PROTOS * jnp.dot(row_weight, expo_tab, precision=lax.Precision.HIGHEST))
        if sweep + 1 < ITERS:
            row_weight = 1.0 / (SAMPLES * jnp.dot(expo_tab, col_scale, precision=lax.Precision.HIGHEST))
    weighted = expo_tab * col_scale[None, :]
    targets = weighted / lax.optimization_barrier(jnp.sum(weighted, axis=1, keepdims=True))
    stud_all = jnp.concatenate([unit_rows[:TEACH_FIRST], unit_rows[teach_end:]], axis=0)
    index_all = jnp.concatenate([crop_sample[:TEACH_FIRST], crop_sample[teach_end:]], axis=0)
    live_all = jnp.concatenate([crop_live[:TEACH_FIRST], crop_live[teach_end:]], axis=0)
    stud_units = stud_all.reshape(-1, ROWS_DEV, WIDTH)
    stud_index = index_all.reshape(-1, ROWS_DEV).astype(jnp.int32)
    stud_live = live_all.reshape(-1, ROWS_DEV).astype(jnp.float32)

    def one_block(operands):
        unit_block, index_block, live_block = operands
        stud_logits = jnp.dot(unit_block, prototypes, preferred_element_type=jnp.float32) / STUD_TEMP
        stud_top = lax.optimization_barrier(jnp.max(stud_logits, axis=1, keepdims=True))
        log_total = stud_top[:, 0] + jnp.log(lax.optimization_barrier(jnp.sum(jnp.exp(stud_logits - stud_top), axis=1)))
        stud_probs = jnp.exp(stud_logits - log_total[:, None])
        chosen = jnp.take(targets, index_block, axis=0)
        loss_block = live_block * (log_total - lax.optimization_barrier(jnp.sum(chosen * stud_logits, axis=1)))
        prob_gap = (live_block[:, None] * (stud_probs - chosen)).astype(jnp.bfloat16)
        grad_block = lax.dot_general(prob_gap, prototypes, (((1,), (1,)), ((), ())), preferred_element_type=jnp.float32) / STUD_TEMP
        return (loss_block, grad_block)
    losses, grads = lax.map(one_block, (stud_units, stud_index, stud_live))
    losses = losses.reshape(-1)
    grads = grads.reshape(-1, WIDTH)
    crop_loss = jnp.concatenate([losses[:TEACH_FIRST], jnp.zeros((SAMPLES,), jnp.float32), losses[TEACH_FIRST:]], axis=0)
    embed_grad = jnp.concatenate([grads[:TEACH_FIRST], jnp.zeros((SAMPLES, WIDTH), jnp.float32), grads[TEACH_FIRST:]], axis=0)
    return (crop_loss, embed_grad)
```

```python
import functools
import math

import jax
import jax.numpy as jnp
from jax import lax
from jax.experimental import pallas as pl
from jax.experimental.pallas import tpu as pltpu
from jax.sharding import PartitionSpec as P

ITERS = 3
TEACH_TEMP = 0.07
STUD_TEMP = 0.1
LOG2E = math.log2(math.e)
LOW = -1e30
AXES = ("sec", "proto")
VMEM_LIMIT = 50 * 1024 * 1024


def unit_rows_of(features):
    values = features.astype(jnp.float32)
    scaled = values * lax.rsqrt(jnp.sum(values * values, axis=1, keepdims=True) + 1e-06)
    return scaled.astype(jnp.bfloat16)


def teacher_kernel(steps, sec_ref, rows_ref, proto_ref, expo_ref, top_ref, dots, top):
    step = pl.program_id(0)
    chunk = proto_ref.shape[1]

    @pl.when(step == 0)
    def _():
        top[...] = jnp.full_like(top, LOW)

    @pl.when(step < steps)
    def _():
        part = jnp.dot(rows_ref[...], proto_ref[...], preferred_element_type=jnp.float32)
        dots[step] = part
        top[...] = jnp.maximum(top[...], jnp.max(part, axis=1, keepdims=True))

    @pl.when(step >= steps)
    def _():
        shifted = dots[step - steps] - top[...]
        expo_ref[...] = jnp.exp2(shifted * (LOG2E / TEACH_TEMP)).astype(jnp.bfloat16)
        top_ref[...] = top[...]


def teacher_expo(sec_index, rows, prototypes, cols, chunk):
    count, width = rows.shape
    steps = cols // chunk
    return pl.pallas_call(
        functools.partial(teacher_kernel, steps),
        out_shape=(
            jax.ShapeDtypeStruct((count, cols), jnp.bfloat16),
            jax.ShapeDtypeStruct((count, 1), jnp.float32),
        ),
        grid_spec=pltpu.PrefetchScalarGridSpec(
            num_scalar_prefetch=1,
            grid=(2 * steps,),
            in_specs=[
                pl.BlockSpec((count, width), lambda s, sec: (0, 0)),
                pl.BlockSpec(
                    (width, chunk), lambda s, sec: (0, sec[0] * steps + jnp.minimum(s, steps - 1))
                ),
            ],
            out_specs=[
                pl.BlockSpec((count, chunk), lambda s, sec: (0, jnp.maximum(s - steps, 0))),
                pl.BlockSpec((count, 1), lambda s, sec: (0, 0)),
            ],
            scratch_shapes=[
                pltpu.VMEM((steps, count, chunk), jnp.float32),
                pltpu.VMEM((count, 1), jnp.float32),
            ],
        ),
        compiler_params=pltpu.CompilerParams(vmem_limit_bytes=VMEM_LIMIT),
        cost_estimate=pl.CostEstimate(
            flops=2 * count * width * cols, bytes_accessed=4 * width * cols, transcendentals=0
        ),
    )(sec_index, rows, prototypes)


def lanes_sum(block):
    total = block[:, 0:128]
    for at in range(128, block.shape[1], 128):
        total = total + block[:, at : at + 128]
    return total


def sweep_kernel(protos, factor_ref, weight_ref, expo_ref, total_ref, partial):
    step = pl.program_id(0)

    @pl.when(step == 0)
    def _():
        partial[...] = jnp.zeros_like(partial)

    expo = expo_ref[...].astype(jnp.float32) * factor_ref[...]
    col_total = jnp.sum(expo * weight_ref[...], axis=0, keepdims=True)
    col_scale = 1.0 / (protos * col_total)
    partial[...] += lanes_sum(expo * col_scale)
    total_ref[...] = jnp.sum(partial[...], axis=1, keepdims=True)


def sweep(factor, weight, expo_tab, protos, chunk):
    count, cols = expo_tab.shape
    return pl.pallas_call(
        functools.partial(sweep_kernel, protos),
        out_shape=jax.ShapeDtypeStruct((count, 1), jnp.float32),
        grid=(cols // chunk,),
        in_specs=[
            pl.BlockSpec((count, 1), lambda s: (0, 0)),
            pl.BlockSpec((count, 1), lambda s: (0, 0)),
            pl.BlockSpec((count, chunk), lambda s: (0, s)),
        ],
        out_specs=pl.BlockSpec((count, 1), lambda s: (0, 0)),
        scratch_shapes=[pltpu.VMEM((count, 128), jnp.float32)],
        compiler_params=pltpu.CompilerParams(vmem_limit_bytes=VMEM_LIMIT),
        cost_estimate=pl.CostEstimate(
            flops=6 * count * cols, bytes_accessed=2 * count * cols, transcendentals=0
        ),
    )(factor, weight, expo_tab)


def mean_kernel(protos, sec_ref, factor_ref, weight_ref, expo_ref, proto_ref, mean_ref, total_ref, partial):
    step = pl.program_id(0)

    @pl.when(step == 0)
    def _():
        partial[...] = jnp.zeros_like(partial)
        mean_ref[...] = jnp.zeros_like(mean_ref)

    expo = expo_ref[...].astype(jnp.float32) * factor_ref[...]
    col_total = jnp.sum(expo * weight_ref[...], axis=0, keepdims=True)
    col_scale = 1.0 / (protos * col_total)
    target = (expo * col_scale).astype(jnp.bfloat16)
    partial[...] += lanes_sum(target.astype(jnp.float32))
    total_ref[...] = jnp.sum(partial[...], axis=1, keepdims=True)
    mean_ref[...] += lax.dot_general(
        target, proto_ref[...], (((1,), (1,)), ((), ())), preferred_element_type=jnp.float32
    )


def target_mean(sec_index, factor, weight, expo_tab, prototypes, protos, chunk):
    count, cols = expo_tab.shape
    width = prototypes.shape[0]
    steps = cols // chunk
    return pl.pallas_call(
        functools.partial(mean_kernel, protos),
        out_shape=(
            jax.ShapeDtypeStruct((count, width), jnp.float32),
            jax.ShapeDtypeStruct((count, 1), jnp.float32),
        ),
        grid_spec=pltpu.PrefetchScalarGridSpec(
            num_scalar_prefetch=1,
            grid=(steps,),
            in_specs=[
                pl.BlockSpec((count, 1), lambda s, sec: (0, 0)),
                pl.BlockSpec((count, 1), lambda s, sec: (0, 0)),
                pl.BlockSpec((count, chunk), lambda s, sec: (0, s)),
                pl.BlockSpec((width, chunk), lambda s, sec: (0, sec[0] * steps + s)),
            ],
            out_specs=[
                pl.BlockSpec((count, width), lambda s, sec: (0, 0)),
                pl.BlockSpec((count, 1), lambda s, sec: (0, 0)),
            ],
            scratch_shapes=[pltpu.VMEM((count, 128), jnp.float32)],
        ),
        compiler_params=pltpu.CompilerParams(vmem_limit_bytes=VMEM_LIMIT),
        cost_estimate=pl.CostEstimate(
            flops=2 * count * width * cols, bytes_accessed=4 * width * cols, transcendentals=0
        ),
    )(sec_index, factor, weight, expo_tab, prototypes)


def student_kernel(sec_ref, rows_ref, now_ref, before_ref, grad_ref, top_ref, total_ref, dots, top, partial):
    step = pl.program_id(0)

    @pl.when(step == 0)
    def _():
        dots[1] = jnp.full(dots.shape[1:], LOW, jnp.float32)
        top[...] = jnp.full_like(top, 2 * LOW)
        partial[...] = jnp.zeros_like(partial)
        grad_ref[...] = jnp.zeros_like(grad_ref)

    slot = lax.rem(step, 2)
    dots[slot] = jnp.dot(rows_ref[...], now_ref[...], preferred_element_type=jnp.float32)
    before = dots[1 - slot]
    old_top = top[...]
    new_top = jnp.maximum(old_top, jnp.max(before, axis=1, keepdims=True))
    expo = jnp.exp2((before - new_top) * (LOG2E / STUD_TEMP))
    shrink = jnp.exp2((old_top - new_top) * (LOG2E / STUD_TEMP))
    top[...] = new_top
    partial[...] = partial[...] * shrink + lanes_sum(expo)
    grad_ref[...] = grad_ref[...] * shrink + lax.dot_general(
        expo.astype(jnp.bfloat16),
        before_ref[...],
        (((1,), (1,)), ((), ())),
        preferred_element_type=jnp.float32,
    )
    top_ref[...] = new_top
    total_ref[...] = jnp.sum(partial[...], axis=1, keepdims=True)


def student_mean(sec_index, rows, prototypes, cols, chunk):
    count, width = rows.shape
    steps = cols // chunk
    return pl.pallas_call(
        student_kernel,
        out_shape=(
            jax.ShapeDtypeStruct((count, width), jnp.float32),
            jax.ShapeDtypeStruct((count, 1), jnp.float32),
            jax.ShapeDtypeStruct((count, 1), jnp.float32),
        ),
        grid_spec=pltpu.PrefetchScalarGridSpec(
            num_scalar_prefetch=1,
            grid=(steps + 1,),
            in_specs=[
                pl.BlockSpec((count, width), lambda s, sec: (0, 0)),
                pl.BlockSpec(
                    (width, chunk), lambda s, sec: (0, sec[0] * steps + jnp.minimum(s, steps - 1))
                ),
                pl.BlockSpec(
                    (width, chunk), lambda s, sec: (0, sec[0] * steps + jnp.maximum(s - 1, 0))
                ),
            ],
            out_specs=[
                pl.BlockSpec((count, width), lambda s, sec: (0, 0)),
                pl.BlockSpec((count, 1), lambda s, sec: (0, 0)),
                pl.BlockSpec((count, 1), lambda s, sec: (0, 0)),
            ],
            scratch_shapes=[
                pltpu.VMEM((2, count, chunk), jnp.float32),
                pltpu.VMEM((count, 1), jnp.float32),
                pltpu.VMEM((count, 128), jnp.float32),
            ],
        ),
        compiler_params=pltpu.CompilerParams(vmem_limit_bytes=VMEM_LIMIT),
        cost_estimate=pl.CostEstimate(
            flops=4 * count * width * cols, bytes_accessed=4 * width * cols, transcendentals=0
        ),
    )(sec_index, rows, prototypes, prototypes)


def halve(blocks, axis):
    size = lax.axis_size(axis)
    index = lax.axis_index(axis)
    bit = 1
    while bit < size:
        rows, width = blocks.shape[1:]
        pairs = blocks.reshape(-1, 2, rows, width)
        mine = lax.rem(index // bit, 2)
        keep = lax.dynamic_index_in_dim(pairs, mine, 1, keepdims=False)
        give = lax.dynamic_index_in_dim(pairs, 1 - mine, 1, keepdims=False)
        got = lax.ppermute(
            give.astype(jnp.bfloat16), axis, [(i, i ^ bit) for i in range(size)]
        )
        blocks = keep + got.astype(jnp.float32)
        bit *= 2
    return blocks[0]


def per_device(features, prototypes, crop_sample, crop_live):
    row_count, width = features.shape
    proto_devs = lax.axis_size("proto")
    sec_devs = lax.axis_size("sec")
    teach_devs = sec_devs // 4
    first_dev = sec_devs // 2 - teach_devs // 2
    sample_count = row_count * teach_devs
    cols = prototypes.shape[1] // sec_devs
    protos = prototypes.shape[1] * proto_devs
    chunk = math.gcd(cols, 1024)
    sec_index = lax.axis_index("sec")
    sec_array = sec_index.astype(jnp.int32).reshape(1)
    is_student = jnp.logical_or(sec_index < first_dev, sec_index >= first_dev + teach_devs)

    own_rows = unit_rows_of(features)
    all_rows = lax.all_gather(own_rows, "sec", axis=0, tiled=True)
    teach_rows = all_rows[first_dev * row_count : first_dev * row_count + sample_count]
    expo_tab, local_top = teacher_expo(sec_array, teach_rows, prototypes, cols, chunk)
    row_top = lax.pmax(local_top, AXES)
    factor = jnp.exp2((local_top - row_top) * (LOG2E / TEACH_TEMP))
    weight = jnp.ones_like(factor)
    for _ in range(ITERS - 1):
        row_total = lax.psum(sweep(factor, weight, expo_tab, protos, chunk), AXES)
        weight = 1.0 / (sample_count * row_total)
    target_sums, target_total = target_mean(
        sec_array, factor, weight, expo_tab, prototypes, protos, chunk
    )
    target_sums, target_total = lax.psum((target_sums, target_total), AXES)
    targets_mean = target_sums / target_total

    parts, tops, totals = [], [], []
    for sec in range(sec_devs):
        if first_dev <= sec < first_dev + teach_devs:
            continue
        rows = all_rows[sec * row_count : (sec + 1) * row_count]
        part, top, total = student_mean(sec_array, rows, prototypes, cols, chunk)
        parts.append(part)
        tops.append(top)
        totals.append(total)
    tops = jnp.stack(tops)
    global_top = lax.pmax(tops, AXES)
    shrink = jnp.exp2((tops - global_top) * (LOG2E / STUD_TEMP))
    all_totals = lax.psum(jnp.stack(totals) * shrink, AXES)
    blank = jnp.zeros((teach_devs, row_count, width), jnp.float32)
    scaled = jnp.stack(parts) * shrink
    blocks = jnp.concatenate([scaled[:first_dev], blank, scaled[first_dev:]], axis=0)
    block = halve(blocks, "sec")
    stud_sums = halve(block.reshape(proto_devs, row_count // proto_devs, width), "proto")

    place = jnp.where(sec_index < first_dev, sec_index, sec_index - teach_devs)
    place = jnp.where(is_student, place, 0)
    own_top = lax.dynamic_index_in_dim(global_top, place, 0, keepdims=False)
    own_total = lax.dynamic_index_in_dim(all_totals, place, 0, keepdims=False)
    log_total = (own_top / STUD_TEMP + jnp.log(own_total))[:, 0]
    live = crop_live.astype(jnp.float32) * is_student.astype(jnp.float32)
    sample = jnp.where(is_student, crop_sample, 0)
    chosen = jnp.take(targets_mean, sample, axis=0)
    cross = jnp.sum(own_rows.astype(jnp.float32) * chosen, axis=1) / STUD_TEMP
    crop_loss = jnp.where(live > 0, live * (log_total - cross), 0.0)

    out_rows = row_count // proto_devs
    start = lax.axis_index("proto") * out_rows
    my_total = lax.dynamic_slice_in_dim(own_total, start, out_rows, 0)
    my_chosen = lax.dynamic_slice_in_dim(chosen, start, out_rows, 0)
    my_live = lax.dynamic_slice_in_dim(live, start, out_rows, 0)[:, None]
    gap = stud_sums / my_total - my_chosen
    embed_grad = jnp.where(my_live > 0, my_live * gap / STUD_TEMP, 0.0)
    return (crop_loss, embed_grad)


def solution(mesh):
    in_specs = (P("sec", None), P(None, "proto"), P("sec"), P("sec"))
    out_specs = (P("sec"), P(("sec", "proto"), None))
    return jax.shard_map(
        per_device, mesh=mesh, in_specs=in_specs, out_specs=out_specs, check_vma=False
    )
```

```python
import functools
import math

import jax
import jax.numpy as jnp
from jax import lax
from jax.experimental import pallas as pl
from jax.experimental.pallas import tpu as pltpu
from jax.sharding import PartitionSpec as P

ITERS = 3
TEACH_TEMP = 0.07
STUD_TEMP = 0.1
LOG2E = math.log2(math.e)
LOW = -1e30
AXES = ("sec", "proto")
VMEM_LIMIT = 50 * 1024 * 1024


def unit_rows_of(features):
    values = features.astype(jnp.float32)
    scaled = values * lax.rsqrt(jnp.sum(values * values, axis=1, keepdims=True) + 1e-06)
    return scaled.astype(jnp.bfloat16)


def teacher_kernel(rows_ref_sec, rows_ref, proto_ref, expo_ref, top_ref):
    count = rows_ref.shape[0]
    half = count // 2
    parts = [
        jnp.dot(rows_ref[at : at + half], proto_ref[...], preferred_element_type=jnp.float32)
        for at in (0, half)
    ]
    for at, part in zip((0, half), parts):
        top = jnp.max(part, axis=1, keepdims=True)
        top_ref[0, at : at + half] = top
        expo_ref[at : at + half] = jnp.exp2((part - top) * (LOG2E / TEACH_TEMP)).astype(
            jnp.bfloat16
        )


def teacher_expo(sec_index, rows, prototypes, cols, chunk):
    count, width = rows.shape
    steps = cols // chunk
    return pl.pallas_call(
        teacher_kernel,
        out_shape=(
            jax.ShapeDtypeStruct((count, cols), jnp.bfloat16),
            jax.ShapeDtypeStruct((steps, count, 1), jnp.float32),
        ),
        grid_spec=pltpu.PrefetchScalarGridSpec(
            num_scalar_prefetch=1,
            grid=(steps,),
            in_specs=[
                pl.BlockSpec((count, width), lambda s, sec: (0, 0)),
                pl.BlockSpec((width, chunk), lambda s, sec: (0, sec[0] * steps + s)),
            ],
            out_specs=[
                pl.BlockSpec((count, chunk), lambda s, sec: (0, s)),
                pl.BlockSpec((1, count, 1), lambda s, sec: (s, 0, 0)),
            ],
        ),
        compiler_params=pltpu.CompilerParams(vmem_limit_bytes=VMEM_LIMIT),
        cost_estimate=pl.CostEstimate(
            flops=2 * count * width * cols, bytes_accessed=4 * width * cols, transcendentals=0
        ),
    )(sec_index, rows, prototypes)


def lanes_sum(block):
    total = block[:, 0:128]
    for at in range(128, block.shape[1], 128):
        total = total + block[:, at : at + 128]
    return total


def sweep_kernel(protos, factor_ref, weight_ref, expo_ref, total_ref, partial):
    step = pl.program_id(0)

    @pl.when(step == 0)
    def _():
        partial[...] = jnp.zeros_like(partial)

    expo = expo_ref[...].astype(jnp.float32) * factor_ref[0]
    col_total = jnp.sum(expo * weight_ref[...], axis=0, keepdims=True)
    col_scale = 1.0 / (protos * col_total)
    partial[...] += lanes_sum(expo * col_scale)
    total_ref[...] = jnp.sum(partial[...], axis=1, keepdims=True)


def sweep(factor, weight, expo_tab, protos, chunk):
    count, cols = expo_tab.shape
    return pl.pallas_call(
        functools.partial(sweep_kernel, protos),
        out_shape=jax.ShapeDtypeStruct((count, 1), jnp.float32),
        grid=(cols // chunk,),
        in_specs=[
            pl.BlockSpec((1, count, 1), lambda s: (s, 0, 0)),
            pl.BlockSpec((count, 1), lambda s: (0, 0)),
            pl.BlockSpec((count, chunk), lambda s: (0, s)),
        ],
        out_specs=pl.BlockSpec((count, 1), lambda s: (0, 0)),
        scratch_shapes=[pltpu.VMEM((count, 128), jnp.float32)],
        compiler_params=pltpu.CompilerParams(vmem_limit_bytes=VMEM_LIMIT),
        cost_estimate=pl.CostEstimate(
            flops=6 * count * cols, bytes_accessed=2 * count * cols, transcendentals=0
        ),
    )(factor, weight, expo_tab)


def mean_kernel(protos, sec_ref, factor_ref, weight_ref, expo_ref, proto_ref, mean_ref, total_ref, partial):
    step = pl.program_id(0)

    @pl.when(step == 0)
    def _():
        partial[...] = jnp.zeros_like(partial)
        mean_ref[...] = jnp.zeros_like(mean_ref)

    expo = expo_ref[...].astype(jnp.float32) * factor_ref[0]
    col_total = jnp.sum(expo * weight_ref[...], axis=0, keepdims=True)
    col_scale = 1.0 / (protos * col_total)
    target = (expo * col_scale).astype(jnp.bfloat16)
    partial[...] += lanes_sum(target.astype(jnp.float32))
    total_ref[...] = jnp.sum(partial[...], axis=1, keepdims=True)
    mean_ref[...] += lax.dot_general(
        target, proto_ref[...], (((1,), (1,)), ((), ())), preferred_element_type=jnp.float32
    )


def target_mean(sec_index, factor, weight, expo_tab, prototypes, protos, chunk):
    count, cols = expo_tab.shape
    width = prototypes.shape[0]
    steps = cols // chunk
    return pl.pallas_call(
        functools.partial(mean_kernel, protos),
        out_shape=(
            jax.ShapeDtypeStruct((count, width), jnp.float32),
            jax.ShapeDtypeStruct((count, 1), jnp.float32),
        ),
        grid_spec=pltpu.PrefetchScalarGridSpec(
            num_scalar_prefetch=1,
            grid=(steps,),
            in_specs=[
                pl.BlockSpec((1, count, 1), lambda s, sec: (s, 0, 0)),
                pl.BlockSpec((count, 1), lambda s, sec: (0, 0)),
                pl.BlockSpec((count, chunk), lambda s, sec: (0, s)),
                pl.BlockSpec((width, chunk), lambda s, sec: (0, sec[0] * steps + s)),
            ],
            out_specs=[
                pl.BlockSpec((count, width), lambda s, sec: (0, 0)),
                pl.BlockSpec((count, 1), lambda s, sec: (0, 0)),
            ],
            scratch_shapes=[pltpu.VMEM((count, 128), jnp.float32)],
        ),
        compiler_params=pltpu.CompilerParams(vmem_limit_bytes=VMEM_LIMIT),
        cost_estimate=pl.CostEstimate(
            flops=2 * count * width * cols, bytes_accessed=4 * width * cols, transcendentals=0
        ),
    )(sec_index, factor, weight, expo_tab, prototypes)


def student_kernel(block, sec_ref, rows_ref, proto_ref, grad_ref, top_ref, total_ref, partial):
    step = pl.program_id(0)

    @pl.when(step == 0)
    def _():
        top_ref[...] = jnp.full_like(top_ref, LOW)
        partial[...] = jnp.zeros_like(partial)
        grad_ref[...] = jnp.zeros_like(grad_ref)

    def dots_of(at):
        return jnp.dot(
            rows_ref[at : at + block], proto_ref[...], preferred_element_type=jnp.float32
        )

    starts = list(range(0, rows_ref.shape[0], block))
    ahead = dots_of(starts[0])
    for turn, at in enumerate(starts):
        dots = ahead
        if turn + 1 < len(starts):
            ahead = dots_of(starts[turn + 1])
        old_top = top_ref[at : at + block]
        new_top = jnp.maximum(old_top, jnp.max(dots, axis=1, keepdims=True))
        expo = jnp.exp2((dots - new_top) * (LOG2E / STUD_TEMP))
        shrink = jnp.exp2((old_top - new_top) * (LOG2E / STUD_TEMP))
        top_ref[at : at + block] = new_top
        partial[at : at + block] = partial[at : at + block] * shrink + lanes_sum(expo)
        grad_ref[at : at + block] = grad_ref[at : at + block] * shrink + lax.dot_general(
            expo.astype(jnp.bfloat16),
            proto_ref[...],
            (((1,), (1,)), ((), ())),
            preferred_element_type=jnp.float32,
        )

    @pl.when(step == pl.num_programs(0) - 1)
    def _():
        total_ref[...] = jnp.sum(partial[...], axis=1, keepdims=True)


def student_mean(sec_index, rows, prototypes, cols, chunk, block):
    count, width = rows.shape
    steps = cols // chunk
    return pl.pallas_call(
        functools.partial(student_kernel, block),
        out_shape=(
            jax.ShapeDtypeStruct((count, width), jnp.float32),
            jax.ShapeDtypeStruct((count, 1), jnp.float32),
            jax.ShapeDtypeStruct((count, 1), jnp.float32),
        ),
        grid_spec=pltpu.PrefetchScalarGridSpec(
            num_scalar_prefetch=1,
            grid=(steps,),
            in_specs=[
                pl.BlockSpec((count, width), lambda s, sec: (0, 0)),
                pl.BlockSpec((width, chunk), lambda s, sec: (0, sec[0] * steps + s)),
            ],
            out_specs=[
                pl.BlockSpec((count, width), lambda s, sec: (0, 0)),
                pl.BlockSpec((count, 1), lambda s, sec: (0, 0)),
                pl.BlockSpec((count, 1), lambda s, sec: (0, 0)),
            ],
            scratch_shapes=[pltpu.VMEM((count, 128), jnp.float32)],
        ),
        compiler_params=pltpu.CompilerParams(vmem_limit_bytes=VMEM_LIMIT),
        cost_estimate=pl.CostEstimate(
            flops=4 * count * width * cols, bytes_accessed=4 * width * cols, transcendentals=0
        ),
    )(sec_index, rows, prototypes)


def share_kernel(combine, sizes, value_ref, out_ref, *scratch):
    slots = scratch[: len(AXES)]
    send_sems, recv_sems = scratch[len(AXES) :]
    barrier = pltpu.get_barrier_semaphore()
    peers = 0
    for axis, size in zip(AXES, sizes):
        me = lax.axis_index(axis)
        for shift in range(1, size):
            pl.semaphore_signal(
                barrier,
                inc=1,
                device_id={axis: lax.rem(me + shift, size)},
                device_id_type=pl.DeviceIdType.MESH,
            )
            peers += 1
    pl.semaphore_wait(barrier, peers)
    current = value_ref[...]
    number = 0
    for axis, size, slot in zip(AXES, sizes, slots):
        me = lax.axis_index(axis)
        slot[me] = current
        copies = []
        for shift in range(1, size):
            copy = pltpu.make_async_remote_copy(
                src_ref=slot.at[me],
                dst_ref=slot.at[me],
                send_sem=send_sems.at[number],
                recv_sem=recv_sems.at[number],
                device_id={axis: lax.rem(me + shift, size)},
                device_id_type=pl.DeviceIdType.MESH,
            )
            copy.start()
            copies.append(copy)
            number += 1
        for copy in copies:
            copy.wait()
        current = slot[0]
        for other in range(1, size):
            current = combine(current, slot[other])
    out_ref[...] = current


def share(combine, vectors, collective_id):
    sizes = tuple(lax.axis_size(axis) for axis in AXES)
    flat = jnp.concatenate([vector.reshape(-1) for vector in vectors])
    count = flat.shape[0]
    rows = -(-count // 1024) * 8
    flat = jnp.pad(flat, (0, rows * 128 - count)).reshape(rows, 128)
    peers = sum(sizes) - len(sizes)
    shared = pl.pallas_call(
        functools.partial(share_kernel, combine, sizes),
        out_shape=jax.ShapeDtypeStruct((rows, 128), jnp.float32),
        in_specs=[pl.BlockSpec(memory_space=pltpu.VMEM)],
        out_specs=pl.BlockSpec(memory_space=pltpu.VMEM),
        scratch_shapes=[pltpu.VMEM((size, rows, 128), jnp.float32) for size in sizes]
        + [pltpu.SemaphoreType.DMA((peers,)), pltpu.SemaphoreType.DMA((peers,))],
        compiler_params=pltpu.CompilerParams(collective_id=collective_id, has_side_effects=True),
    )(flat).reshape(-1)
    results, at = [], 0
    for vector in vectors:
        results.append(shared[at : at + vector.size].reshape(vector.shape))
        at += vector.size
    return results


def halve(blocks, axis):
    size = lax.axis_size(axis)
    index = lax.axis_index(axis)
    bit = 1
    while bit < size:
        rows, width = blocks.shape[1:]
        pairs = blocks.reshape(-1, 2, rows, width)
        mine = lax.rem(index // bit, 2)
        keep = lax.dynamic_index_in_dim(pairs, mine, 1, keepdims=False)
        give = lax.dynamic_index_in_dim(pairs, 1 - mine, 1, keepdims=False)
        got = lax.ppermute(
            give.astype(jnp.bfloat16), axis, [(i, i ^ bit) for i in range(size)]
        )
        blocks = keep + got.astype(jnp.float32)
        bit *= 2
    return blocks[0]


def per_device(features, prototypes, crop_sample, crop_live):
    row_count, width = features.shape
    proto_devs = lax.axis_size("proto")
    sec_devs = lax.axis_size("sec")
    teach_devs = sec_devs // 4
    first_dev = sec_devs // 2 - teach_devs // 2
    sample_count = row_count * teach_devs
    cols = prototypes.shape[1] // sec_devs
    protos = prototypes.shape[1] * proto_devs
    chunk = math.gcd(cols, 2048)
    sec_index = lax.axis_index("sec")
    sec_array = sec_index.astype(jnp.int32).reshape(1)
    is_student = jnp.logical_or(sec_index < first_dev, sec_index >= first_dev + teach_devs)

    own_rows = unit_rows_of(features)
    sample = jnp.where(is_student, crop_sample, 0)
    digits = jnp.concatenate([sample // 128, sample % 128]).astype(jnp.bfloat16)
    extra = -(-digits.shape[0] // (16 * width)) * 16
    digits = jnp.pad(digits, (0, extra * width - digits.shape[0])).reshape(extra, width)
    packed = lax.all_gather(jnp.concatenate([own_rows, digits]), "sec", axis=0)
    all_rows = packed[:, :row_count]
    all_digits = packed[:, row_count:].reshape(sec_devs, -1)[:, : 2 * row_count].astype(jnp.int32)
    all_samples = all_digits[:, :row_count] * 128 + all_digits[:, row_count:]

    def students_of(blocks):
        return jnp.concatenate([blocks[:first_dev], blocks[first_dev + teach_devs :]])

    stud_rows = students_of(all_rows).reshape(-1, width)
    stud_samples = students_of(all_samples).reshape(-1)
    teach_rows = all_rows[first_dev : first_dev + teach_devs].reshape(-1, width)

    stud_part, stud_top, stud_total = student_mean(
        sec_array, stud_rows, prototypes, cols, chunk, row_count
    )
    expo_tab, chunk_tops = teacher_expo(sec_array, teach_rows, prototypes, cols, chunk)
    row_top, global_top = share(jnp.maximum, [jnp.max(chunk_tops, axis=0), stud_top], 0)
    factor = jnp.exp2((chunk_tops - row_top) * (LOG2E / TEACH_TEMP))
    weight = jnp.ones_like(row_top)
    for turn in range(ITERS - 1):
        row_part = sweep(factor, weight, expo_tab, protos, chunk)
        (row_total,) = share(jnp.add, [row_part], 1 + turn)
        weight = 1.0 / (sample_count * row_total)
    target_part, target_total = target_mean(
        sec_array, factor, weight, expo_tab, prototypes, protos, chunk
    )
    pick = (stud_samples[:, None] == jnp.arange(sample_count)[None, :]).astype(jnp.bfloat16)
    chosen_part = jnp.dot(
        pick, target_part.astype(jnp.bfloat16), preferred_element_type=jnp.float32
    )
    cross_part = jnp.sum(stud_rows.astype(jnp.float32) * chosen_part, axis=1, keepdims=True)
    shrink = jnp.exp2((stud_top - global_top) * (LOG2E / STUD_TEMP))
    target_total, stud_total, cross = share(
        jnp.add, [target_total, stud_total * shrink, cross_part], ITERS
    )
    chosen_total = jnp.take(target_total[:, 0], stud_samples)[:, None]
    gap_part = stud_part * (shrink / stud_total) - chosen_part / chosen_total
    gap_part = gap_part.reshape(-1, row_count, width)
    blank = jnp.zeros((teach_devs, row_count, width), jnp.float32)
    blocks = jnp.concatenate([gap_part[:first_dev], blank, gap_part[first_dev:]])
    block = halve(blocks, "sec")
    gap = halve(block.reshape(proto_devs, row_count // proto_devs, width), "proto")

    loss = global_top / STUD_TEMP + jnp.log(stud_total) - cross / chosen_total / STUD_TEMP
    place = jnp.where(sec_index < first_dev, sec_index, sec_index - teach_devs)
    place = jnp.where(is_student, place, 0)
    own_loss = lax.dynamic_index_in_dim(loss.reshape(-1, row_count), place, 0, keepdims=False)
    live = crop_live.astype(jnp.float32) * is_student.astype(jnp.float32)
    crop_loss = jnp.where(live > 0, live * own_loss, 0.0)
    out_rows = row_count // proto_devs
    start = lax.axis_index("proto") * out_rows
    my_live = lax.dynamic_slice_in_dim(live, start, out_rows, 0)[:, None]
    embed_grad = jnp.where(my_live > 0, my_live * gap / STUD_TEMP, 0.0)
    return (crop_loss, embed_grad)


def solution(mesh):
    in_specs = (P("sec", None), P(None, "proto"), P("sec"), P("sec"))
    out_specs = (P("sec"), P(("sec", "proto"), None))
    return jax.shard_map(
        per_device, mesh=mesh, in_specs=in_specs, out_specs=out_specs, check_vma=False
    )
```

```python
import functools
import math

import jax
import jax.numpy as jnp
from jax import lax
from jax.experimental import pallas as pl
from jax.experimental.pallas import tpu as pltpu
from jax.sharding import PartitionSpec as P

ITERS = 3
TEACH_TEMP = 0.07
STUD_TEMP = 0.1
LOG2E = math.log2(math.e)
LOW = -1e30
AXES = ("sec", "proto")
VMEM_LIMIT = 50 * 1024 * 1024


def unit_rows_of(features):
    values = features.astype(jnp.float32)
    scaled = values * lax.rsqrt(jnp.sum(values * values, axis=1, keepdims=True) + 1e-06)
    return scaled.astype(jnp.bfloat16)


def teacher_kernel(rows_ref_sec, rows_ref, proto_ref, expo_ref, top_ref):
    count = rows_ref.shape[0]
    half = count // 2
    parts = [
        jnp.dot(rows_ref[at : at + half], proto_ref[...], preferred_element_type=jnp.float32)
        for at in (0, half)
    ]
    for at, part in zip((0, half), parts):
        top = jnp.max(part, axis=1, keepdims=True)
        top_ref[0, at : at + half] = top
        expo_ref[at : at + half] = jnp.exp2((part - top) * (LOG2E / TEACH_TEMP)).astype(
            jnp.bfloat16
        )


def teacher_expo(sec_index, rows, prototypes, cols, chunk):
    count, width = rows.shape
    steps = cols // chunk
    return pl.pallas_call(
        teacher_kernel,
        out_shape=(
            jax.ShapeDtypeStruct((count, cols), jnp.bfloat16),
            jax.ShapeDtypeStruct((steps, count, 1), jnp.float32),
        ),
        grid_spec=pltpu.PrefetchScalarGridSpec(
            num_scalar_prefetch=1,
            grid=(steps,),
            in_specs=[
                pl.BlockSpec((count, width), lambda s, sec: (0, 0)),
                pl.BlockSpec((width, chunk), lambda s, sec: (0, sec[0] * steps + s)),
            ],
            out_specs=[
                pl.BlockSpec((count, chunk), lambda s, sec: (0, s)),
                pl.BlockSpec((1, count, 1), lambda s, sec: (s, 0, 0)),
            ],
        ),
        compiler_params=pltpu.CompilerParams(vmem_limit_bytes=VMEM_LIMIT),
        cost_estimate=pl.CostEstimate(
            flops=2 * count * width * cols, bytes_accessed=4 * width * cols, transcendentals=0
        ),
    )(sec_index, rows, prototypes)


def lanes_sum(block):
    total = block[:, 0:128]
    for at in range(128, block.shape[1], 128):
        total = total + block[:, at : at + 128]
    return total


def sweep_kernel(protos, factor_ref, weight_ref, expo_ref, total_ref, partial):
    step = pl.program_id(0)

    @pl.when(step == 0)
    def _():
        partial[...] = jnp.zeros_like(partial)

    expo = expo_ref[...].astype(jnp.float32) * factor_ref[0]
    col_total = jnp.sum(expo * weight_ref[...], axis=0, keepdims=True)
    col_scale = 1.0 / (protos * col_total)
    partial[...] += lanes_sum(expo * col_scale)
    total_ref[...] = jnp.sum(partial[...], axis=1, keepdims=True)


def sweep(factor, weight, expo_tab, protos, chunk):
    count, cols = expo_tab.shape
    return pl.pallas_call(
        functools.partial(sweep_kernel, protos),
        out_shape=jax.ShapeDtypeStruct((count, 1), jnp.float32),
        grid=(cols // chunk,),
        in_specs=[
            pl.BlockSpec((1, count, 1), lambda s: (s, 0, 0)),
            pl.BlockSpec((count, 1), lambda s: (0, 0)),
            pl.BlockSpec((count, chunk), lambda s: (0, s)),
        ],
        out_specs=pl.BlockSpec((count, 1), lambda s: (0, 0)),
        scratch_shapes=[pltpu.VMEM((count, 128), jnp.float32)],
        compiler_params=pltpu.CompilerParams(vmem_limit_bytes=VMEM_LIMIT),
        cost_estimate=pl.CostEstimate(
            flops=6 * count * cols, bytes_accessed=2 * count * cols, transcendentals=0
        ),
    )(factor, weight, expo_tab)


def mean_kernel(protos, sec_ref, factor_ref, weight_ref, expo_ref, proto_ref, mean_ref, total_ref, partial):
    step = pl.program_id(0)

    @pl.when(step == 0)
    def _():
        partial[...] = jnp.zeros_like(partial)
        mean_ref[...] = jnp.zeros_like(mean_ref)

    expo = expo_ref[...].astype(jnp.float32) * factor_ref[0]
    col_total = jnp.sum(expo * weight_ref[...], axis=0, keepdims=True)
    col_scale = 1.0 / (protos * col_total)
    target = (expo * col_scale).astype(jnp.bfloat16)
    partial[...] += lanes_sum(target.astype(jnp.float32))
    total_ref[...] = jnp.sum(partial[...], axis=1, keepdims=True)
    mean_ref[...] += lax.dot_general(
        target, proto_ref[...], (((1,), (1,)), ((), ())), preferred_element_type=jnp.float32
    )


def target_mean(sec_index, factor, weight, expo_tab, prototypes, protos, chunk):
    count, cols = expo_tab.shape
    width = prototypes.shape[0]
    steps = cols // chunk
    return pl.pallas_call(
        functools.partial(mean_kernel, protos),
        out_shape=(
            jax.ShapeDtypeStruct((count, width), jnp.float32),
            jax.ShapeDtypeStruct((count, 1), jnp.float32),
        ),
        grid_spec=pltpu.PrefetchScalarGridSpec(
            num_scalar_prefetch=1,
            grid=(steps,),
            in_specs=[
                pl.BlockSpec((1, count, 1), lambda s, sec: (s, 0, 0)),
                pl.BlockSpec((count, 1), lambda s, sec: (0, 0)),
                pl.BlockSpec((count, chunk), lambda s, sec: (0, s)),
                pl.BlockSpec((width, chunk), lambda s, sec: (0, sec[0] * steps + s)),
            ],
            out_specs=[
                pl.BlockSpec((count, width), lambda s, sec: (0, 0)),
                pl.BlockSpec((count, 1), lambda s, sec: (0, 0)),
            ],
            scratch_shapes=[pltpu.VMEM((count, 128), jnp.float32)],
        ),
        compiler_params=pltpu.CompilerParams(vmem_limit_bytes=VMEM_LIMIT),
        cost_estimate=pl.CostEstimate(
            flops=2 * count * width * cols, bytes_accessed=4 * width * cols, transcendentals=0
        ),
    )(sec_index, factor, weight, expo_tab, prototypes)


def fold(combine):
    def run(values):
        total = values[0]
        for value in values[1:]:
            total = combine(total, value)
        return total

    return run


def fold_softmax(top_rows):
    def run(values):
        tops = [value[:top_rows] for value in values]
        highest = fold(jnp.maximum)(tops)
        totals = fold(jnp.add)(
            [
                value[top_rows : 2 * top_rows] * jnp.exp2((top - highest) * (LOG2E / STUD_TEMP))
                for value, top in zip(values, tops)
            ]
        )
        return jnp.concatenate(
            [highest, totals, fold(jnp.add)([value[2 * top_rows :] for value in values])]
        )

    return run


class Exchange:
    def __init__(self, sizes, combine, slots, send_sems, recv_sems):
        self.sizes, self.combine, self.slots = sizes, combine, slots
        self.send_sems, self.recv_sems = send_sems, recv_sems

    def greet(self):
        barrier = pltpu.get_barrier_semaphore()
        for axis, size in zip(AXES, self.sizes):
            me = lax.axis_index(axis)
            for shift in range(1, size):
                pl.semaphore_signal(
                    barrier,
                    inc=1,
                    device_id={axis: lax.rem(me + shift, size)},
                    device_id_type=pl.DeviceIdType.MESH,
                )

    def wait_greetings(self):
        pl.semaphore_wait(pltpu.get_barrier_semaphore(), sum(self.sizes) - len(self.sizes))

    def copies(self, turn):
        size = self.sizes[turn]
        me = lax.axis_index(AXES[turn])
        first = sum(self.sizes[:turn]) - turn
        return [
            pltpu.make_async_remote_copy(
                src_ref=self.slots[turn].at[me],
                dst_ref=self.slots[turn].at[me],
                send_sem=self.send_sems.at[first + shift - 1],
                recv_sem=self.recv_sems.at[first + shift - 1],
                device_id={AXES[turn]: lax.rem(me + shift, size)},
                device_id_type=pl.DeviceIdType.MESH,
            )
            for shift in range(1, size)
        ]

    def send(self, turn, value):
        self.slots[turn][lax.axis_index(AXES[turn])] = value
        for copy in self.copies(turn):
            copy.start()

    def collect(self, turn):
        for copy in self.copies(turn):
            copy.wait()
        return self.combine([self.slots[turn][other] for other in range(self.sizes[turn])])


def exchange_scratch(sizes, rows):
    peers = sum(sizes) - len(sizes)
    return [pltpu.VMEM((size, rows, 128), jnp.float32) for size in sizes] + [
        pltpu.SemaphoreType.DMA((peers,)),
        pltpu.SemaphoreType.DMA((peers,)),
    ]


def pack(vectors):
    pieces = []
    for vector in vectors:
        flat = vector.reshape(-1)
        pieces.append(jnp.pad(flat, (0, -flat.shape[0] % 1024)).reshape(-1, 128))
    return jnp.concatenate(pieces)


def unpack(shared, vectors):
    results, at = [], 0
    for vector in vectors:
        rows = -(-vector.size // 1024) * 8
        flat = shared[at : at + rows].reshape(-1)[: vector.size]
        results.append(flat.reshape(vector.shape))
        at += rows
    return results


def share_kernel(sizes, combine, value_ref, out_ref, sec_slot, proto_slot, send_sems, recv_sems):
    exchange = Exchange(sizes, combine, (sec_slot, proto_slot), send_sems, recv_sems)
    exchange.greet()
    exchange.wait_greetings()
    exchange.send(0, value_ref[...])
    exchange.send(1, exchange.collect(0))
    out_ref[...] = exchange.collect(1)


def share(combine, vectors, collective_id):
    sizes = tuple(lax.axis_size(axis) for axis in AXES)
    packed = pack(vectors)
    shared = pl.pallas_call(
        functools.partial(share_kernel, sizes, combine),
        out_shape=jax.ShapeDtypeStruct(packed.shape, jnp.float32),
        in_specs=[pl.BlockSpec(memory_space=pltpu.VMEM)],
        out_specs=pl.BlockSpec(memory_space=pltpu.VMEM),
        scratch_shapes=exchange_scratch(sizes, packed.shape[0]),
        compiler_params=pltpu.CompilerParams(collective_id=collective_id, has_side_effects=True),
    )(packed)
    return unpack(shared, vectors)


def student_kernel(
    steps, unit, sizes, combine,
    rows_ref, value_ref, proto_ref,
    grad_ref, top_ref, total_ref, shared_ref,
    partial, sec_slot, proto_slot, send_sems, recv_sems,
):
    step = pl.program_id(0)
    exchange = Exchange(sizes, combine, (sec_slot, proto_slot), send_sems, recv_sems)

    @pl.when(step == 0)
    def _():
        exchange.greet()
        top_ref[...] = jnp.full_like(top_ref, LOW)
        partial[...] = jnp.zeros_like(partial)
        grad_ref[...] = jnp.zeros_like(grad_ref)

    @pl.when(step == min(1, steps - 1))
    def _():
        exchange.wait_greetings()
        exchange.send(0, value_ref[...])

    @pl.when(step == min(2, steps - 1))
    def _():
        exchange.send(1, exchange.collect(0))

    def dots_of(at):
        return jnp.dot(
            rows_ref[...], proto_ref[:, at : at + unit], preferred_element_type=jnp.float32
        )

    starts = list(range(0, proto_ref.shape[1], unit))
    ahead = dots_of(starts[0])
    for turn, at in enumerate(starts):
        dots = ahead
        if turn + 1 < len(starts):
            ahead = dots_of(starts[turn + 1])
        old_top = top_ref[...]
        new_top = jnp.maximum(old_top, jnp.max(dots, axis=1, keepdims=True))
        expo = jnp.exp2((dots - new_top) * (LOG2E / STUD_TEMP))
        shrink = jnp.exp2((old_top - new_top) * (LOG2E / STUD_TEMP))
        top_ref[...] = new_top
        partial[...] = partial[...] * shrink + lanes_sum(expo)
        grad_ref[...] = grad_ref[...] * shrink + lax.dot_general(
            expo.astype(jnp.bfloat16),
            proto_ref[:, at : at + unit],
            (((1,), (1,)), ((), ())),
            preferred_element_type=jnp.float32,
        )

    @pl.when(step == steps - 1)
    def _():
        total_ref[...] = jnp.sum(partial[...], axis=1, keepdims=True)
        shared_ref[...] = exchange.collect(1)


def student_mean(rows, prototypes, cols, chunk, combine, vectors, collective_id):
    count, width = rows.shape
    steps = cols // chunk
    sizes = tuple(lax.axis_size(axis) for axis in AXES)
    packed = pack(vectors)
    part, top, total, shared = pl.pallas_call(
        functools.partial(student_kernel, steps, math.gcd(chunk, 1024), sizes, combine),
        out_shape=(
            jax.ShapeDtypeStruct((count, width), jnp.float32),
            jax.ShapeDtypeStruct((count, 1), jnp.float32),
            jax.ShapeDtypeStruct((count, 1), jnp.float32),
            jax.ShapeDtypeStruct(packed.shape, jnp.float32),
        ),
        grid=(steps,),
        in_specs=[
            pl.BlockSpec((count, width), lambda s: (0, 0)),
            pl.BlockSpec(packed.shape, lambda s: (0, 0)),
            pl.BlockSpec((width, chunk), lambda s: (0, lax.axis_index("sec") * steps + s)),
        ],
        out_specs=[
            pl.BlockSpec((count, width), lambda s: (0, 0)),
            pl.BlockSpec((count, 1), lambda s: (0, 0)),
            pl.BlockSpec((count, 1), lambda s: (0, 0)),
            pl.BlockSpec(packed.shape, lambda s: (0, 0)),
        ],
        scratch_shapes=[pltpu.VMEM((count, 128), jnp.float32)]
        + exchange_scratch(sizes, packed.shape[0]),
        compiler_params=pltpu.CompilerParams(
            vmem_limit_bytes=VMEM_LIMIT, collective_id=collective_id, has_side_effects=True
        ),
        cost_estimate=pl.CostEstimate(
            flops=4 * count * width * cols, bytes_accessed=4 * width * cols, transcendentals=0
        ),
    )(rows, packed, prototypes)
    return part, top, total, unpack(shared, vectors)


def halve(blocks, order):
    for axis, bit in order:
        size, dim = lax.axis_size(axis), AXES.index(axis)
        mine = lax.rem(lax.axis_index(axis) // bit, 2)
        shape = blocks.shape
        pairs = blocks.reshape(shape[:dim] + (shape[dim] // 2, 2) + shape[dim + 1 :])
        keep = lax.dynamic_index_in_dim(pairs, mine, dim + 1, keepdims=False)
        give = lax.dynamic_index_in_dim(pairs, 1 - mine, dim + 1, keepdims=False)
        got = lax.ppermute(
            give.astype(jnp.bfloat16), axis, [(i, i ^ bit) for i in range(size)]
        )
        blocks = keep + got.astype(jnp.float32)
    return blocks[0, 0]


def bits_of(axis):
    return [(axis, 1 << at) for at in range(lax.axis_size(axis).bit_length() - 1)]


def per_device(features, prototypes, crop_sample, crop_live):
    row_count, width = features.shape
    proto_devs = lax.axis_size("proto")
    sec_devs = lax.axis_size("sec")
    teach_devs = sec_devs // 4
    first_dev = sec_devs // 2 - teach_devs // 2
    sample_count = row_count * teach_devs
    cols = prototypes.shape[1] // sec_devs
    protos = prototypes.shape[1] * proto_devs
    chunk = math.gcd(cols, 2048)
    sec_index = lax.axis_index("sec")
    sec_array = sec_index.astype(jnp.int32).reshape(1)
    is_student = jnp.logical_or(sec_index < first_dev, sec_index >= first_dev + teach_devs)

    own_rows = unit_rows_of(features)
    sample = jnp.where(is_student, crop_sample, 0)
    digits = jnp.concatenate([sample // 128, sample % 128]).astype(jnp.bfloat16)
    extra = -(-digits.shape[0] // (16 * width)) * 16
    digits = jnp.pad(digits, (0, extra * width - digits.shape[0])).reshape(extra, width)
    packed = lax.all_gather(jnp.concatenate([own_rows, digits]), "sec", axis=0)
    all_rows = packed[:, :row_count]
    all_digits = packed[:, row_count:].reshape(sec_devs, -1)[:, : 2 * row_count].astype(jnp.int32)
    all_samples = all_digits[:, :row_count] * 128 + all_digits[:, row_count:]

    def students_of(blocks):
        return jnp.concatenate([blocks[:first_dev], blocks[first_dev + teach_devs :]])

    stud_rows = students_of(all_rows).reshape(-1, width)
    stud_samples = students_of(all_samples).reshape(-1)
    teach_rows = all_rows[first_dev : first_dev + teach_devs].reshape(-1, width)

    expo_tab, chunk_tops = teacher_expo(sec_array, teach_rows, prototypes, cols, chunk)
    groups = stud_rows.reshape(ITERS, -1, width)
    found = []
    top_part = jnp.max(chunk_tops, axis=0)
    part, top, total, (row_top,) = student_mean(
        groups[0], prototypes, cols, chunk, fold(jnp.maximum), [top_part], 0
    )
    found.append((part, top, total))
    factor = jnp.exp2((chunk_tops - row_top) * (LOG2E / TEACH_TEMP))
    weight = jnp.ones_like(row_top)
    for turn in range(1, ITERS):
        row_part = sweep(factor, weight, expo_tab, protos, chunk)
        part, top, total, (row_total,) = student_mean(
            groups[turn], prototypes, cols, chunk, fold(jnp.add), [row_part], turn
        )
        found.append((part, top, total))
        weight = 1.0 / (sample_count * row_total)
    stud_part, stud_top, stud_total = [jnp.concatenate(pieces) for pieces in zip(*found)]
    target_part, target_total = target_mean(
        sec_array, factor, weight, expo_tab, prototypes, protos, chunk
    )
    pick = (stud_samples[:, None] == jnp.arange(sample_count)[None, :]).astype(jnp.bfloat16)
    chosen_part = jnp.dot(
        pick, target_part.astype(jnp.bfloat16), preferred_element_type=jnp.float32
    )
    cross_part = jnp.sum(stud_rows.astype(jnp.float32) * chosen_part, axis=1, keepdims=True)
    global_top, stud_total, target_total, cross = share(
        fold_softmax(-(-stud_top.size // 1024) * 8),
        [stud_top, stud_total, target_total, cross_part],
        ITERS,
    )
    shrink = jnp.exp2((stud_top - global_top) * (LOG2E / STUD_TEMP))
    chosen_total = jnp.sum(
        jnp.where(pick > 0, target_total.reshape(1, -1), 0.0), axis=1, keepdims=True
    )
    gap_part = stud_part * (shrink / stud_total) - chosen_part / chosen_total
    gap_part = gap_part.reshape(-1, row_count, width)
    blank = jnp.zeros((teach_devs, row_count, width), jnp.float32)
    blocks = jnp.concatenate([gap_part[:first_dev], blank, gap_part[first_dev:]])
    blocks = blocks.reshape(sec_devs, proto_devs, row_count // proto_devs, width)
    over_sec, over_proto = bits_of("sec"), bits_of("proto")
    one = halve(blocks[..., : width // 2], over_sec + over_proto)
    two = halve(
        blocks[..., width // 2 :], over_sec[:1] + over_proto[:1] + over_sec[1:] + over_proto[1:]
    )
    gap = jnp.concatenate([one, two], axis=1)

    loss = global_top / STUD_TEMP + jnp.log(stud_total) - cross / chosen_total / STUD_TEMP
    place = jnp.where(sec_index < first_dev, sec_index, sec_index - teach_devs)
    place = jnp.where(is_student, place, 0)
    own_loss = lax.dynamic_index_in_dim(loss.reshape(-1, row_count), place, 0, keepdims=False)
    live = crop_live.astype(jnp.float32) * is_student.astype(jnp.float32)
    crop_loss = jnp.where(live > 0, live * own_loss, 0.0)
    out_rows = row_count // proto_devs
    start = lax.axis_index("proto") * out_rows
    my_live = lax.dynamic_slice_in_dim(live, start, out_rows, 0)[:, None]
    embed_grad = jnp.where(my_live > 0, my_live * gap / STUD_TEMP, 0.0)
    return (crop_loss, embed_grad)


def solution(mesh):
    in_specs = (P("sec", None), P(None, "proto"), P("sec"), P("sec"))
    out_specs = (P("sec"), P(("sec", "proto"), None))
    return jax.shard_map(
        per_device, mesh=mesh, in_specs=in_specs, out_specs=out_specs, check_vma=False
    )
```

```python
import functools
import math

import jax
import jax.numpy as jnp
from jax import lax
from jax.experimental import pallas as pl
from jax.experimental.pallas import tpu as pltpu
from jax.sharding import PartitionSpec as P

ITERS = 3
TEACH_TEMP = 0.07
STUD_TEMP = 0.1
LOG2E = math.log2(math.e)
LOW = -1e30
AXES = ("sec", "proto")
VMEM_LIMIT = 50 * 1024 * 1024


def unit_rows_of(features):
    values = features.astype(jnp.float32)
    scaled = values * lax.rsqrt(jnp.sum(values * values, axis=1, keepdims=True) + 1e-06)
    return scaled.astype(jnp.bfloat16)


def gather_kernel(size, own_ref, all_ref, local_sem, send_sems, recv_sems):
    me, place = lax.axis_index("sec"), lax.axis_index("proto")
    core, line, lines = lax.rem(me, 2), me // 2, size // 2
    half = lax.rem(place, 2)
    rows = own_ref.shape[0] // 2
    mine = pl.ds(pl.multiple_of(half * rows, 16), rows)
    rest = pl.ds(pl.multiple_of((1 - half) * rows, 16), rows)
    other_core = {"sec": me + 1 - 2 * core}
    neighbour = {"proto": place + 1 - 2 * half}
    across = [{"sec": lax.rem(line + k, lines) * 2 + core} for k in range(1, lines)]
    source = [lax.rem(line - k + lines, lines) * 2 + core for k in range(1, lines)]
    barrier = pltpu.get_barrier_semaphore()
    for target in [other_core, neighbour] + across:
        pl.semaphore_signal(
            barrier, inc=1, device_id=target, device_id_type=pl.DeviceIdType.MESH
        )
    pl.semaphore_wait(barrier, lines + 1)

    def copy_to(number, src, dst, target):
        return pltpu.make_async_remote_copy(
            src_ref=src,
            dst_ref=dst,
            send_sem=send_sems.at[number],
            recv_sem=recv_sems.at[number],
            device_id=target,
            device_id_type=pl.DeviceIdType.MESH,
        )

    outer = [
        copy_to(k, own_ref.at[mine], all_ref.at[me, mine], target)
        for k, target in enumerate(across)
    ]
    for copy in outer:
        copy.start()
    whole = copy_to(4 * (lines - 1), own_ref, all_ref.at[me], other_core)
    whole.start()
    local = pltpu.make_async_copy(own_ref, all_ref.at[me], local_sem)
    local.start()
    sides, firsts, seconds = [], [], []
    for k, block in enumerate(source):
        outer[k].wait_recv()
        piece = all_ref.at[block, mine]
        side = copy_to(lines - 1 + k, piece, piece, neighbour)
        first = copy_to(2 * (lines - 1) + k, piece, piece, other_core)
        side.start()
        first.start()
        sides.append(side)
        firsts.append(first)
    for k, block in enumerate(source):
        sides[k].wait_recv()
        piece = all_ref.at[block, rest]
        second = copy_to(3 * (lines - 1) + k, piece, piece, other_core)
        second.start()
        seconds.append(second)
    local.wait()
    whole.wait()
    for copy in outer + sides:
        copy.wait_send()
    for copy in firsts + seconds:
        copy.wait()


def gather_rows(own, collective_id):
    size = lax.axis_size("sec")
    copies = 4 * (size // 2 - 1) + 1
    return pl.pallas_call(
        functools.partial(gather_kernel, size),
        out_shape=jax.ShapeDtypeStruct((size,) + own.shape, own.dtype),
        in_specs=[pl.BlockSpec(memory_space=pl.ANY)],
        out_specs=pl.BlockSpec(memory_space=pl.ANY),
        scratch_shapes=[
            pltpu.SemaphoreType.DMA,
            pltpu.SemaphoreType.DMA((copies,)),
            pltpu.SemaphoreType.DMA((copies,)),
        ],
        compiler_params=pltpu.CompilerParams(collective_id=collective_id, has_side_effects=True),
    )(own)


def teacher_kernel(rows_ref_sec, rows_ref, proto_ref, expo_ref, top_ref):
    count = rows_ref.shape[0]
    half = count // 2
    parts = [
        jnp.dot(rows_ref[at : at + half], proto_ref[...], preferred_element_type=jnp.float32)
        for at in (0, half)
    ]
    for at, part in zip((0, half), parts):
        top = jnp.max(part, axis=1, keepdims=True)
        top_ref[0, at : at + half] = top
        expo_ref[at : at + half] = jnp.exp2((part - top) * (LOG2E / TEACH_TEMP)).astype(
            jnp.bfloat16
        )


def teacher_expo(sec_index, rows, prototypes, cols, chunk):
    count, width = rows.shape
    steps = cols // chunk
    return pl.pallas_call(
        teacher_kernel,
        out_shape=(
            jax.ShapeDtypeStruct((count, cols), jnp.bfloat16),
            jax.ShapeDtypeStruct((steps, count, 1), jnp.float32),
        ),
        grid_spec=pltpu.PrefetchScalarGridSpec(
            num_scalar_prefetch=1,
            grid=(steps,),
            in_specs=[
                pl.BlockSpec((count, width), lambda s, sec: (0, 0)),
                pl.BlockSpec((width, chunk), lambda s, sec: (0, sec[0] * steps + s)),
            ],
            out_specs=[
                pl.BlockSpec((count, chunk), lambda s, sec: (0, s)),
                pl.BlockSpec((1, count, 1), lambda s, sec: (s, 0, 0)),
            ],
        ),
        compiler_params=pltpu.CompilerParams(vmem_limit_bytes=VMEM_LIMIT),
        cost_estimate=pl.CostEstimate(
            flops=2 * count * width * cols, bytes_accessed=4 * width * cols, transcendentals=0
        ),
    )(sec_index, rows, prototypes)


def lanes_sum(block):
    total = block[:, 0:128]
    for at in range(128, block.shape[1], 128):
        total = total + block[:, at : at + 128]
    return total


def sweep_kernel(protos, factor_ref, weight_ref, expo_ref, total_ref, partial):
    step = pl.program_id(0)

    @pl.when(step == 0)
    def _():
        partial[...] = jnp.zeros_like(partial)

    expo = expo_ref[...].astype(jnp.float32) * factor_ref[0]
    col_total = jnp.sum(expo * weight_ref[...], axis=0, keepdims=True)
    col_scale = 1.0 / (protos * col_total)
    partial[...] += lanes_sum(expo * col_scale)
    total_ref[...] = jnp.sum(partial[...], axis=1, keepdims=True)


def sweep(factor, weight, expo_tab, protos, chunk):
    count, cols = expo_tab.shape
    return pl.pallas_call(
        functools.partial(sweep_kernel, protos),
        out_shape=jax.ShapeDtypeStruct((count, 1), jnp.float32),
        grid=(cols // chunk,),
        in_specs=[
            pl.BlockSpec((1, count, 1), lambda s: (s, 0, 0)),
            pl.BlockSpec((count, 1), lambda s: (0, 0)),
            pl.BlockSpec((count, chunk), lambda s: (0, s)),
        ],
        out_specs=pl.BlockSpec((count, 1), lambda s: (0, 0)),
        scratch_shapes=[pltpu.VMEM((count, 128), jnp.float32)],
        compiler_params=pltpu.CompilerParams(vmem_limit_bytes=VMEM_LIMIT),
        cost_estimate=pl.CostEstimate(
            flops=6 * count * cols, bytes_accessed=2 * count * cols, transcendentals=0
        ),
    )(factor, weight, expo_tab)


def mean_kernel(protos, sec_ref, factor_ref, weight_ref, expo_ref, proto_ref, mean_ref, total_ref, partial):
    step = pl.program_id(0)

    @pl.when(step == 0)
    def _():
        partial[...] = jnp.zeros_like(partial)
        mean_ref[...] = jnp.zeros_like(mean_ref)

    expo = expo_ref[...].astype(jnp.float32) * factor_ref[0]
    col_total = jnp.sum(expo * weight_ref[...], axis=0, keepdims=True)
    col_scale = 1.0 / (protos * col_total)
    target = (expo * col_scale).astype(jnp.bfloat16)
    partial[...] += lanes_sum(target.astype(jnp.float32))
    total_ref[...] = jnp.sum(partial[...], axis=1, keepdims=True)
    mean_ref[...] += lax.dot_general(
        target, proto_ref[...], (((1,), (1,)), ((), ())), preferred_element_type=jnp.float32
    )


def target_mean(sec_index, factor, weight, expo_tab, prototypes, protos, chunk):
    count, cols = expo_tab.shape
    width = prototypes.shape[0]
    steps = cols // chunk
    return pl.pallas_call(
        functools.partial(mean_kernel, protos),
        out_shape=(
            jax.ShapeDtypeStruct((count, width), jnp.float32),
            jax.ShapeDtypeStruct((count, 1), jnp.float32),
        ),
        grid_spec=pltpu.PrefetchScalarGridSpec(
            num_scalar_prefetch=1,
            grid=(steps,),
            in_specs=[
                pl.BlockSpec((1, count, 1), lambda s, sec: (s, 0, 0)),
                pl.BlockSpec((count, 1), lambda s, sec: (0, 0)),
                pl.BlockSpec((count, chunk), lambda s, sec: (0, s)),
                pl.BlockSpec((width, chunk), lambda s, sec: (0, sec[0] * steps + s)),
            ],
            out_specs=[
                pl.BlockSpec((count, width), lambda s, sec: (0, 0)),
                pl.BlockSpec((count, 1), lambda s, sec: (0, 0)),
            ],
            scratch_shapes=[pltpu.VMEM((count, 128), jnp.float32)],
        ),
        compiler_params=pltpu.CompilerParams(vmem_limit_bytes=VMEM_LIMIT),
        cost_estimate=pl.CostEstimate(
            flops=2 * count * width * cols, bytes_accessed=4 * width * cols, transcendentals=0
        ),
    )(sec_index, factor, weight, expo_tab, prototypes)


def fold(combine):
    def run(values):
        total = values[0]
        for value in values[1:]:
            total = combine(total, value)
        return total

    return run


def fold_softmax(top_rows):
    def run(values):
        tops = [value[:top_rows] for value in values]
        highest = fold(jnp.maximum)(tops)
        totals = fold(jnp.add)(
            [
                value[top_rows : 2 * top_rows] * jnp.exp2((top - highest) * (LOG2E / STUD_TEMP))
                for value, top in zip(values, tops)
            ]
        )
        return jnp.concatenate(
            [highest, totals, fold(jnp.add)([value[2 * top_rows :] for value in values])]
        )

    return run


class Exchange:
    def __init__(self, sizes, combine, slots, send_sems, recv_sems):
        self.sizes, self.combine, self.slots = sizes, combine, slots
        self.send_sems, self.recv_sems = send_sems, recv_sems

    def greet(self):
        barrier = pltpu.get_barrier_semaphore()
        for axis, size in zip(AXES, self.sizes):
            me = lax.axis_index(axis)
            for shift in range(1, size):
                pl.semaphore_signal(
                    barrier,
                    inc=1,
                    device_id={axis: lax.rem(me + shift, size)},
                    device_id_type=pl.DeviceIdType.MESH,
                )

    def wait_greetings(self):
        pl.semaphore_wait(pltpu.get_barrier_semaphore(), sum(self.sizes) - len(self.sizes))

    def copies(self, turn):
        size = self.sizes[turn]
        me = lax.axis_index(AXES[turn])
        first = sum(self.sizes[:turn]) - turn
        return [
            pltpu.make_async_remote_copy(
                src_ref=self.slots[turn].at[me],
                dst_ref=self.slots[turn].at[me],
                send_sem=self.send_sems.at[first + shift - 1],
                recv_sem=self.recv_sems.at[first + shift - 1],
                device_id={AXES[turn]: lax.rem(me + shift, size)},
                device_id_type=pl.DeviceIdType.MESH,
            )
            for shift in range(1, size)
        ]

    def send(self, turn, value):
        self.slots[turn][lax.axis_index(AXES[turn])] = value
        for copy in self.copies(turn):
            copy.start()

    def collect(self, turn):
        for copy in self.copies(turn):
            copy.wait()
        return self.combine([self.slots[turn][other] for other in range(self.sizes[turn])])


def exchange_scratch(sizes, rows):
    peers = sum(sizes) - len(sizes)
    return [pltpu.VMEM((size, rows, 128), jnp.float32) for size in sizes] + [
        pltpu.SemaphoreType.DMA((peers,)),
        pltpu.SemaphoreType.DMA((peers,)),
    ]


def pack(vectors):
    pieces = []
    for vector in vectors:
        flat = vector.reshape(-1)
        pieces.append(jnp.pad(flat, (0, -flat.shape[0] % 1024)).reshape(-1, 128))
    return jnp.concatenate(pieces)


def unpack(shared, vectors):
    results, at = [], 0
    for vector in vectors:
        rows = -(-vector.size // 1024) * 8
        flat = shared[at : at + rows].reshape(-1)[: vector.size]
        results.append(flat.reshape(vector.shape))
        at += rows
    return results


def share_kernel(sizes, combine, value_ref, out_ref, sec_slot, proto_slot, send_sems, recv_sems):
    exchange = Exchange(sizes, combine, (sec_slot, proto_slot), send_sems, recv_sems)
    exchange.greet()
    exchange.wait_greetings()
    exchange.send(0, value_ref[...])
    exchange.send(1, exchange.collect(0))
    out_ref[...] = exchange.collect(1)


def share(combine, vectors, collective_id):
    sizes = tuple(lax.axis_size(axis) for axis in AXES)
    packed = pack(vectors)
    shared = pl.pallas_call(
        functools.partial(share_kernel, sizes, combine),
        out_shape=jax.ShapeDtypeStruct(packed.shape, jnp.float32),
        in_specs=[pl.BlockSpec(memory_space=pltpu.VMEM)],
        out_specs=pl.BlockSpec(memory_space=pltpu.VMEM),
        scratch_shapes=exchange_scratch(sizes, packed.shape[0]),
        compiler_params=pltpu.CompilerParams(collective_id=collective_id, has_side_effects=True),
    )(packed)
    return unpack(shared, vectors)


def student_kernel(
    steps, unit, sizes, combine,
    rows_ref, value_ref, proto_ref,
    grad_ref, top_ref, total_ref, shared_ref,
    partial, sec_slot, proto_slot, send_sems, recv_sems,
):
    step = pl.program_id(0)
    exchange = Exchange(sizes, combine, (sec_slot, proto_slot), send_sems, recv_sems)

    @pl.when(step == 0)
    def _():
        exchange.greet()
        top_ref[...] = jnp.full_like(top_ref, LOW)
        partial[...] = jnp.zeros_like(partial)
        grad_ref[...] = jnp.zeros_like(grad_ref)

    @pl.when(step == min(1, steps - 1))
    def _():
        exchange.wait_greetings()
        exchange.send(0, value_ref[...])

    @pl.when(step == min(2, steps - 1))
    def _():
        exchange.send(1, exchange.collect(0))

    def dots_of(at):
        return jnp.dot(
            rows_ref[...], proto_ref[:, at : at + unit], preferred_element_type=jnp.float32
        )

    starts = list(range(0, proto_ref.shape[1], unit))
    ahead = dots_of(starts[0])
    for turn, at in enumerate(starts):
        dots = ahead
        if turn + 1 < len(starts):
            ahead = dots_of(starts[turn + 1])
        old_top = top_ref[...]
        new_top = jnp.maximum(old_top, jnp.max(dots, axis=1, keepdims=True))
        expo = jnp.exp2((dots - new_top) * (LOG2E / STUD_TEMP))
        shrink = jnp.exp2((old_top - new_top) * (LOG2E / STUD_TEMP))
        top_ref[...] = new_top
        partial[...] = partial[...] * shrink + lanes_sum(expo)
        grad_ref[...] = grad_ref[...] * shrink + lax.dot_general(
            expo.astype(jnp.bfloat16),
            proto_ref[:, at : at + unit],
            (((1,), (1,)), ((), ())),
            preferred_element_type=jnp.float32,
        )

    @pl.when(step == steps - 1)
    def _():
        total_ref[...] = jnp.sum(partial[...], axis=1, keepdims=True)
        shared_ref[...] = exchange.collect(1)


def student_mean(rows, prototypes, cols, chunk, combine, vectors, collective_id):
    count, width = rows.shape
    steps = cols // chunk
    sizes = tuple(lax.axis_size(axis) for axis in AXES)
    packed = pack(vectors)
    part, top, total, shared = pl.pallas_call(
        functools.partial(student_kernel, steps, math.gcd(chunk, 1024), sizes, combine),
        out_shape=(
            jax.ShapeDtypeStruct((count, width), jnp.float32),
            jax.ShapeDtypeStruct((count, 1), jnp.float32),
            jax.ShapeDtypeStruct((count, 1), jnp.float32),
            jax.ShapeDtypeStruct(packed.shape, jnp.float32),
        ),
        grid=(steps,),
        in_specs=[
            pl.BlockSpec((count, width), lambda s: (0, 0)),
            pl.BlockSpec(packed.shape, lambda s: (0, 0)),
            pl.BlockSpec((width, chunk), lambda s: (0, lax.axis_index("sec") * steps + s)),
        ],
        out_specs=[
            pl.BlockSpec((count, width), lambda s: (0, 0)),
            pl.BlockSpec((count, 1), lambda s: (0, 0)),
            pl.BlockSpec((count, 1), lambda s: (0, 0)),
            pl.BlockSpec(packed.shape, lambda s: (0, 0)),
        ],
        scratch_shapes=[pltpu.VMEM((count, 128), jnp.float32)]
        + exchange_scratch(sizes, packed.shape[0]),
        compiler_params=pltpu.CompilerParams(
            vmem_limit_bytes=VMEM_LIMIT, collective_id=collective_id, has_side_effects=True
        ),
        cost_estimate=pl.CostEstimate(
            flops=4 * count * width * cols, bytes_accessed=4 * width * cols, transcendentals=0
        ),
    )(rows, packed, prototypes)
    return part, top, total, unpack(shared, vectors)


def halve(blocks, order):
    for axis, bit in order:
        size, dim = lax.axis_size(axis), AXES.index(axis)
        mine = lax.rem(lax.axis_index(axis) // bit, 2)
        shape = blocks.shape
        pairs = blocks.reshape(shape[:dim] + (shape[dim] // 2, 2) + shape[dim + 1 :])
        keep = lax.dynamic_index_in_dim(pairs, mine, dim + 1, keepdims=False)
        give = lax.dynamic_index_in_dim(pairs, 1 - mine, dim + 1, keepdims=False)
        got = lax.ppermute(
            give.astype(jnp.bfloat16), axis, [(i, i ^ bit) for i in range(size)]
        )
        blocks = keep + got.astype(jnp.float32)
    return blocks[0, 0]


def bits_of(axis):
    return [(axis, 1 << at) for at in range(lax.axis_size(axis).bit_length() - 1)]


def per_device(features, prototypes, crop_sample, crop_live):
    row_count, width = features.shape
    proto_devs = lax.axis_size("proto")
    sec_devs = lax.axis_size("sec")
    teach_devs = sec_devs // 4
    first_dev = sec_devs // 2 - teach_devs // 2
    sample_count = row_count * teach_devs
    cols = prototypes.shape[1] // sec_devs
    protos = prototypes.shape[1] * proto_devs
    chunk = math.gcd(cols, 2048)
    sec_index = lax.axis_index("sec")
    sec_array = sec_index.astype(jnp.int32).reshape(1)
    is_student = jnp.logical_or(sec_index < first_dev, sec_index >= first_dev + teach_devs)

    own_rows = unit_rows_of(features)
    sample = jnp.where(is_student, crop_sample, 0)
    digits = jnp.concatenate([sample // 128, sample % 128]).astype(jnp.bfloat16)
    extra = -(-digits.shape[0] // (32 * width)) * 32
    digits = jnp.pad(digits, (0, extra * width - digits.shape[0])).reshape(extra, width)
    packed = gather_rows(jnp.concatenate([own_rows, digits]), ITERS + 1)
    all_rows = packed[:, :row_count]
    all_digits = packed[:, row_count:].reshape(sec_devs, -1)[:, : 2 * row_count].astype(jnp.int32)
    all_samples = all_digits[:, :row_count] * 128 + all_digits[:, row_count:]

    def students_of(blocks):
        return jnp.concatenate([blocks[:first_dev], blocks[first_dev + teach_devs :]])

    stud_rows = students_of(all_rows).reshape(-1, width)
    stud_samples = students_of(all_samples).reshape(-1)
    teach_rows = all_rows[first_dev : first_dev + teach_devs].reshape(-1, width)

    expo_tab, chunk_tops = teacher_expo(sec_array, teach_rows, prototypes, cols, chunk)
    groups = stud_rows.reshape(ITERS, -1, width)
    found = []
    top_part = jnp.max(chunk_tops, axis=0)
    part, top, total, (row_top,) = student_mean(
        groups[0], prototypes, cols, chunk, fold(jnp.maximum), [top_part], 0
    )
    found.append((part, top, total))
    factor = jnp.exp2((chunk_tops - row_top) * (LOG2E / TEACH_TEMP))
    weight = jnp.ones_like(row_top)
    for turn in range(1, ITERS):
        row_part = sweep(factor, weight, expo_tab, protos, chunk)
        part, top, total, (row_total,) = student_mean(
            groups[turn], prototypes, cols, chunk, fold(jnp.add), [row_part], turn
        )
        found.append((part, top, total))
        weight = 1.0 / (sample_count * row_total)
    stud_part, stud_top, stud_total = [jnp.concatenate(pieces) for pieces in zip(*found)]
    target_part, target_total = target_mean(
        sec_array, factor, weight, expo_tab, prototypes, protos, chunk
    )
    pick = (stud_samples[:, None] == jnp.arange(sample_count)[None, :]).astype(jnp.bfloat16)
    chosen_part = jnp.dot(
        pick, target_part.astype(jnp.bfloat16), preferred_element_type=jnp.float32
    )
    cross_part = jnp.sum(stud_rows.astype(jnp.float32) * chosen_part, axis=1, keepdims=True)
    global_top, stud_total, target_total, cross = share(
        fold_softmax(-(-stud_top.size // 1024) * 8),
        [stud_top, stud_total, target_total, cross_part],
        ITERS,
    )
    shrink = jnp.exp2((stud_top - global_top) * (LOG2E / STUD_TEMP))
    chosen_total = jnp.sum(
        jnp.where(pick > 0, target_total.reshape(1, -1), 0.0), axis=1, keepdims=True
    )
    gap_part = stud_part * (shrink / stud_total) - chosen_part / chosen_total
    gap_part = gap_part.reshape(-1, row_count, width)
    blank = jnp.zeros((teach_devs, row_count, width), jnp.float32)
    blocks = jnp.concatenate([gap_part[:first_dev], blank, gap_part[first_dev:]])
    blocks = blocks.reshape(sec_devs, proto_devs, row_count // proto_devs, width)
    over_sec, over_proto = bits_of("sec"), bits_of("proto")
    one = halve(blocks[..., : width // 2], over_sec + over_proto)
    two = halve(
        blocks[..., width // 2 :], over_sec[:1] + over_proto[:1] + over_sec[1:] + over_proto[1:]
    )
    gap = jnp.concatenate([one, two], axis=1)

    loss = global_top / STUD_TEMP + jnp.log(stud_total) - cross / chosen_total / STUD_TEMP
    place = jnp.where(sec_index < first_dev, sec_index, sec_index - teach_devs)
    place = jnp.where(is_student, place, 0)
    own_loss = lax.dynamic_index_in_dim(loss.reshape(-1, row_count), place, 0, keepdims=False)
    live = crop_live.astype(jnp.float32) * is_student.astype(jnp.float32)
    crop_loss = jnp.where(live > 0, live * own_loss, 0.0)
    out_rows = row_count // proto_devs
    start = lax.axis_index("proto") * out_rows
    my_live = lax.dynamic_slice_in_dim(live, start, out_rows, 0)[:, None]
    embed_grad = jnp.where(my_live > 0, my_live * gap / STUD_TEMP, 0.0)
    return (crop_loss, embed_grad)


def solution(mesh):
    in_specs = (P("sec", None), P(None, "proto"), P("sec"), P("sec"))
    out_specs = (P("sec"), P(("sec", "proto"), None))
    return jax.shard_map(
        per_device, mesh=mesh, in_specs=in_specs, out_specs=out_specs, check_vma=False
    )
```

```python
import functools
import math

import jax
import jax.numpy as jnp
from jax import lax
from jax.experimental import pallas as pl
from jax.experimental.pallas import tpu as pltpu
from jax.sharding import PartitionSpec as P

ITERS = 3
TEACH_TEMP = 0.07
STUD_TEMP = 0.1
LOG2E = math.log2(math.e)
LOW = -1e30
AXES = ("sec", "proto")
VMEM_LIMIT = 50 * 1024 * 1024


def unit_rows_of(features):
    values = features.astype(jnp.float32)
    scaled = values * lax.rsqrt(jnp.sum(values * values, axis=1, keepdims=True) + 1e-06)
    return scaled.astype(jnp.bfloat16)


def gather_kernel(size, own_ref, all_ref, local_sem, send_sems, recv_sems):
    me, place = lax.axis_index("sec"), lax.axis_index("proto")
    core, line, lines = lax.rem(me, 2), me // 2, size // 2
    half = lax.rem(place, 2)
    rows = own_ref.shape[0] // 2
    mine = pl.ds(pl.multiple_of(half * rows, 16), rows)
    rest = pl.ds(pl.multiple_of((1 - half) * rows, 16), rows)
    other_core = {"sec": me + 1 - 2 * core}
    neighbour = {"proto": place + 1 - 2 * half}
    across = [{"sec": lax.rem(line + k, lines) * 2 + core} for k in range(1, lines)]
    source = [lax.rem(line - k + lines, lines) * 2 + core for k in range(1, lines)]
    barrier = pltpu.get_barrier_semaphore()
    for target in [other_core, neighbour] + across:
        pl.semaphore_signal(
            barrier, inc=1, device_id=target, device_id_type=pl.DeviceIdType.MESH
        )
    pl.semaphore_wait(barrier, lines + 1)

    def copy_to(number, src, dst, target):
        return pltpu.make_async_remote_copy(
            src_ref=src,
            dst_ref=dst,
            send_sem=send_sems.at[number],
            recv_sem=recv_sems.at[number],
            device_id=target,
            device_id_type=pl.DeviceIdType.MESH,
        )

    outer = [
        copy_to(k, own_ref.at[mine], all_ref.at[me, mine], target)
        for k, target in enumerate(across)
    ]
    for copy in outer:
        copy.start()
    whole = copy_to(4 * (lines - 1), own_ref, all_ref.at[me], other_core)
    whole.start()
    local = pltpu.make_async_copy(own_ref, all_ref.at[me], local_sem)
    local.start()
    sides, firsts, seconds = [], [], []
    for k, block in enumerate(source):
        outer[k].wait_recv()
        piece = all_ref.at[block, mine]
        side = copy_to(lines - 1 + k, piece, piece, neighbour)
        first = copy_to(2 * (lines - 1) + k, piece, piece, other_core)
        side.start()
        first.start()
        sides.append(side)
        firsts.append(first)
    for k, block in enumerate(source):
        sides[k].wait_recv()
        piece = all_ref.at[block, rest]
        second = copy_to(3 * (lines - 1) + k, piece, piece, other_core)
        second.start()
        seconds.append(second)
    local.wait()
    whole.wait()
    for copy in outer + sides:
        copy.wait_send()
    for copy in firsts + seconds:
        copy.wait()


def gather_rows(own, collective_id):
    size = lax.axis_size("sec")
    copies = 4 * (size // 2 - 1) + 1
    return pl.pallas_call(
        functools.partial(gather_kernel, size),
        out_shape=jax.ShapeDtypeStruct((size,) + own.shape, own.dtype),
        in_specs=[pl.BlockSpec(memory_space=pl.ANY)],
        out_specs=pl.BlockSpec(memory_space=pl.ANY),
        scratch_shapes=[
            pltpu.SemaphoreType.DMA,
            pltpu.SemaphoreType.DMA((copies,)),
            pltpu.SemaphoreType.DMA((copies,)),
        ],
        compiler_params=pltpu.CompilerParams(collective_id=collective_id, has_side_effects=True),
    )(own)


def teacher_kernel(rows_ref_sec, rows_ref, proto_ref, expo_ref, top_ref):
    count = rows_ref.shape[0]
    half = count // 2
    parts = [
        jnp.dot(rows_ref[at : at + half], proto_ref[...], preferred_element_type=jnp.float32)
        for at in (0, half)
    ]
    for at, part in zip((0, half), parts):
        top = jnp.max(part, axis=1, keepdims=True)
        top_ref[0, at : at + half] = top
        expo_ref[at : at + half] = jnp.exp2((part - top) * (LOG2E / TEACH_TEMP)).astype(
            jnp.bfloat16
        )


def teacher_expo(sec_index, rows, prototypes, cols, chunk):
    count, width = rows.shape
    steps = cols // chunk
    return pl.pallas_call(
        teacher_kernel,
        out_shape=(
            jax.ShapeDtypeStruct((count, cols), jnp.bfloat16),
            jax.ShapeDtypeStruct((steps, count, 1), jnp.float32),
        ),
        grid_spec=pltpu.PrefetchScalarGridSpec(
            num_scalar_prefetch=1,
            grid=(steps,),
            in_specs=[
                pl.BlockSpec((count, width), lambda s, sec: (0, 0)),
                pl.BlockSpec((width, chunk), lambda s, sec: (0, sec[0] * steps + s)),
            ],
            out_specs=[
                pl.BlockSpec((count, chunk), lambda s, sec: (0, s)),
                pl.BlockSpec((1, count, 1), lambda s, sec: (s, 0, 0)),
            ],
        ),
        compiler_params=pltpu.CompilerParams(vmem_limit_bytes=VMEM_LIMIT),
        cost_estimate=pl.CostEstimate(
            flops=2 * count * width * cols, bytes_accessed=4 * width * cols, transcendentals=0
        ),
    )(sec_index, rows, prototypes)


def lanes_sum(block):
    total = block[:, 0:128]
    for at in range(128, block.shape[1], 128):
        total = total + block[:, at : at + 128]
    return total


def sweep_kernel(protos, factor_ref, weight_ref, expo_ref, total_ref, partial):
    step = pl.program_id(0)

    @pl.when(step == 0)
    def _():
        partial[...] = jnp.zeros_like(partial)

    expo = expo_ref[...].astype(jnp.float32) * factor_ref[0]
    col_total = jnp.sum(expo * weight_ref[...], axis=0, keepdims=True)
    col_scale = 1.0 / (protos * col_total)
    partial[...] += lanes_sum(expo * col_scale)
    total_ref[...] = jnp.sum(partial[...], axis=1, keepdims=True)


def sweep(factor, weight, expo_tab, protos, chunk):
    count, cols = expo_tab.shape
    return pl.pallas_call(
        functools.partial(sweep_kernel, protos),
        out_shape=jax.ShapeDtypeStruct((count, 1), jnp.float32),
        grid=(cols // chunk,),
        in_specs=[
            pl.BlockSpec((1, count, 1), lambda s: (s, 0, 0)),
            pl.BlockSpec((count, 1), lambda s: (0, 0)),
            pl.BlockSpec((count, chunk), lambda s: (0, s)),
        ],
        out_specs=pl.BlockSpec((count, 1), lambda s: (0, 0)),
        scratch_shapes=[pltpu.VMEM((count, 128), jnp.float32)],
        compiler_params=pltpu.CompilerParams(vmem_limit_bytes=VMEM_LIMIT),
        cost_estimate=pl.CostEstimate(
            flops=6 * count * cols, bytes_accessed=2 * count * cols, transcendentals=0
        ),
    )(factor, weight, expo_tab)


def mean_kernel(protos, sec_ref, factor_ref, weight_ref, expo_ref, proto_ref, mean_ref, total_ref, partial):
    step = pl.program_id(0)

    @pl.when(step == 0)
    def _():
        partial[...] = jnp.zeros_like(partial)
        mean_ref[...] = jnp.zeros_like(mean_ref)

    chunk = expo_ref.shape[1]
    unit = math.gcd(chunk, 512)
    row_part, mean_part = partial[...], mean_ref[...]
    for at in range(0, chunk, unit):
        expo = expo_ref[:, at : at + unit].astype(jnp.float32) * factor_ref[0]
        col_total = jnp.sum(expo * weight_ref[...], axis=0, keepdims=True)
        col_scale = 1.0 / (protos * col_total)
        target = (expo * col_scale).astype(jnp.bfloat16)
        row_part = row_part + lanes_sum(target.astype(jnp.float32))
        mean_part = mean_part + lax.dot_general(
            target,
            proto_ref[:, at : at + unit],
            (((1,), (1,)), ((), ())),
            preferred_element_type=jnp.float32,
        )
    partial[...] = row_part
    mean_ref[...] = mean_part

    @pl.when(step == pl.num_programs(0) - 1)
    def _():
        total_ref[...] = jnp.sum(partial[...], axis=1, keepdims=True)


def target_mean(sec_index, factor, weight, expo_tab, prototypes, protos, chunk):
    count, cols = expo_tab.shape
    width = prototypes.shape[0]
    steps = cols // chunk
    return pl.pallas_call(
        functools.partial(mean_kernel, protos),
        out_shape=(
            jax.ShapeDtypeStruct((count, width), jnp.float32),
            jax.ShapeDtypeStruct((count, 1), jnp.float32),
        ),
        grid_spec=pltpu.PrefetchScalarGridSpec(
            num_scalar_prefetch=1,
            grid=(steps,),
            in_specs=[
                pl.BlockSpec((1, count, 1), lambda s, sec: (s, 0, 0)),
                pl.BlockSpec((count, 1), lambda s, sec: (0, 0)),
                pl.BlockSpec((count, chunk), lambda s, sec: (0, s)),
                pl.BlockSpec((width, chunk), lambda s, sec: (0, sec[0] * steps + s)),
            ],
            out_specs=[
                pl.BlockSpec((count, width), lambda s, sec: (0, 0)),
                pl.BlockSpec((count, 1), lambda s, sec: (0, 0)),
            ],
            scratch_shapes=[pltpu.VMEM((count, 128), jnp.float32)],
        ),
        compiler_params=pltpu.CompilerParams(vmem_limit_bytes=VMEM_LIMIT),
        cost_estimate=pl.CostEstimate(
            flops=2 * count * width * cols, bytes_accessed=4 * width * cols, transcendentals=0
        ),
    )(sec_index, factor, weight, expo_tab, prototypes)


def fold(combine):
    def run(values):
        total = values[0]
        for value in values[1:]:
            total = combine(total, value)
        return total

    return run


def fold_softmax(top_rows):
    def run(values):
        tops = [value[:top_rows] for value in values]
        highest = fold(jnp.maximum)(tops)
        totals = fold(jnp.add)(
            [
                value[top_rows : 2 * top_rows] * jnp.exp2((top - highest) * (LOG2E / STUD_TEMP))
                for value, top in zip(values, tops)
            ]
        )
        return jnp.concatenate(
            [highest, totals, fold(jnp.add)([value[2 * top_rows :] for value in values])]
        )

    return run


class Exchange:
    def __init__(self, sizes, combine, slots, send_sems, recv_sems):
        self.sizes, self.combine, self.slots = sizes, combine, slots
        self.send_sems, self.recv_sems = send_sems, recv_sems

    def greet(self):
        barrier = pltpu.get_barrier_semaphore()
        for axis, size in zip(AXES, self.sizes):
            me = lax.axis_index(axis)
            for shift in range(1, size):
                pl.semaphore_signal(
                    barrier,
                    inc=1,
                    device_id={axis: lax.rem(me + shift, size)},
                    device_id_type=pl.DeviceIdType.MESH,
                )

    def wait_greetings(self):
        pl.semaphore_wait(pltpu.get_barrier_semaphore(), sum(self.sizes) - len(self.sizes))

    def copies(self, turn):
        size = self.sizes[turn]
        me = lax.axis_index(AXES[turn])
        first = sum(self.sizes[:turn]) - turn
        return [
            pltpu.make_async_remote_copy(
                src_ref=self.slots[turn].at[me],
                dst_ref=self.slots[turn].at[me],
                send_sem=self.send_sems.at[first + shift - 1],
                recv_sem=self.recv_sems.at[first + shift - 1],
                device_id={AXES[turn]: lax.rem(me + shift, size)},
                device_id_type=pl.DeviceIdType.MESH,
            )
            for shift in range(1, size)
        ]

    def send(self, turn, value):
        self.slots[turn][lax.axis_index(AXES[turn])] = value
        for copy in self.copies(turn):
            copy.start()

    def collect(self, turn):
        for copy in self.copies(turn):
            copy.wait()
        return self.combine([self.slots[turn][other] for other in range(self.sizes[turn])])


def exchange_scratch(sizes, rows):
    peers = sum(sizes) - len(sizes)
    return [pltpu.VMEM((size, rows, 128), jnp.float32) for size in sizes] + [
        pltpu.SemaphoreType.DMA((peers,)),
        pltpu.SemaphoreType.DMA((peers,)),
    ]


def pack(vectors):
    pieces = []
    for vector in vectors:
        flat = vector.reshape(-1)
        pieces.append(jnp.pad(flat, (0, -flat.shape[0] % 1024)).reshape(-1, 128))
    return jnp.concatenate(pieces)


def unpack(shared, vectors):
    results, at = [], 0
    for vector in vectors:
        rows = -(-vector.size // 1024) * 8
        flat = shared[at : at + rows].reshape(-1)[: vector.size]
        results.append(flat.reshape(vector.shape))
        at += rows
    return results


def share_kernel(sizes, combine, value_ref, out_ref, sec_slot, proto_slot, send_sems, recv_sems):
    exchange = Exchange(sizes, combine, (sec_slot, proto_slot), send_sems, recv_sems)
    exchange.greet()
    exchange.wait_greetings()
    exchange.send(0, value_ref[...])
    exchange.send(1, exchange.collect(0))
    out_ref[...] = exchange.collect(1)


def share(combine, vectors, collective_id):
    sizes = tuple(lax.axis_size(axis) for axis in AXES)
    packed = pack(vectors)
    shared = pl.pallas_call(
        functools.partial(share_kernel, sizes, combine),
        out_shape=jax.ShapeDtypeStruct(packed.shape, jnp.float32),
        in_specs=[pl.BlockSpec(memory_space=pltpu.VMEM)],
        out_specs=pl.BlockSpec(memory_space=pltpu.VMEM),
        scratch_shapes=exchange_scratch(sizes, packed.shape[0]),
        compiler_params=pltpu.CompilerParams(collective_id=collective_id, has_side_effects=True),
    )(packed)
    return unpack(shared, vectors)


def student_kernel(
    steps, unit, sizes, combine,
    rows_ref, value_ref, proto_ref,
    grad_ref, top_ref, total_ref, shared_ref,
    partial, sec_slot, proto_slot, send_sems, recv_sems,
):
    step = pl.program_id(0)
    exchange = Exchange(sizes, combine, (sec_slot, proto_slot), send_sems, recv_sems)

    @pl.when(step == 0)
    def _():
        exchange.greet()
        top_ref[...] = jnp.full_like(top_ref, LOW)
        partial[...] = jnp.zeros_like(partial)
        grad_ref[...] = jnp.zeros_like(grad_ref)

    @pl.when(step == min(1, steps - 1))
    def _():
        exchange.wait_greetings()
        exchange.send(0, value_ref[...])

    @pl.when(step == min(2, steps - 1))
    def _():
        exchange.send(1, exchange.collect(0))

    def dots_of(at):
        return jnp.dot(
            rows_ref[...], proto_ref[:, at : at + unit], preferred_element_type=jnp.float32
        )

    starts = list(range(0, proto_ref.shape[1], unit))
    ahead = dots_of(starts[0])
    for turn, at in enumerate(starts):
        dots = ahead
        if turn + 1 < len(starts):
            ahead = dots_of(starts[turn + 1])
        old_top = top_ref[...]
        new_top = jnp.maximum(old_top, jnp.max(dots, axis=1, keepdims=True))
        expo = jnp.exp2((dots - new_top) * (LOG2E / STUD_TEMP))
        shrink = jnp.exp2((old_top - new_top) * (LOG2E / STUD_TEMP))
        top_ref[...] = new_top
        partial[...] = partial[...] * shrink + lanes_sum(expo)
        grad_ref[...] = grad_ref[...] * shrink + lax.dot_general(
            expo.astype(jnp.bfloat16),
            proto_ref[:, at : at + unit],
            (((1,), (1,)), ((), ())),
            preferred_element_type=jnp.float32,
        )

    @pl.when(step == steps - 1)
    def _():
        total_ref[...] = jnp.sum(partial[...], axis=1, keepdims=True)
        shared_ref[...] = exchange.collect(1)


def student_mean(rows, prototypes, cols, chunk, combine, vectors, collective_id):
    count, width = rows.shape
    steps = cols // chunk
    sizes = tuple(lax.axis_size(axis) for axis in AXES)
    packed = pack(vectors)
    part, top, total, shared = pl.pallas_call(
        functools.partial(student_kernel, steps, math.gcd(chunk, 1024), sizes, combine),
        out_shape=(
            jax.ShapeDtypeStruct((count, width), jnp.float32),
            jax.ShapeDtypeStruct((count, 1), jnp.float32),
            jax.ShapeDtypeStruct((count, 1), jnp.float32),
            jax.ShapeDtypeStruct(packed.shape, jnp.float32),
        ),
        grid=(steps,),
        in_specs=[
            pl.BlockSpec((count, width), lambda s: (0, 0)),
            pl.BlockSpec(packed.shape, lambda s: (0, 0)),
            pl.BlockSpec((width, chunk), lambda s: (0, lax.axis_index("sec") * steps + s)),
        ],
        out_specs=[
            pl.BlockSpec((count, width), lambda s: (0, 0)),
            pl.BlockSpec((count, 1), lambda s: (0, 0)),
            pl.BlockSpec((count, 1), lambda s: (0, 0)),
            pl.BlockSpec(packed.shape, lambda s: (0, 0)),
        ],
        scratch_shapes=[pltpu.VMEM((count, 128), jnp.float32)]
        + exchange_scratch(sizes, packed.shape[0]),
        compiler_params=pltpu.CompilerParams(
            vmem_limit_bytes=VMEM_LIMIT, collective_id=collective_id, has_side_effects=True
        ),
        cost_estimate=pl.CostEstimate(
            flops=4 * count * width * cols, bytes_accessed=4 * width * cols, transcendentals=0
        ),
    )(rows, packed, prototypes)
    return part, top, total, unpack(shared, vectors)


def halve(blocks, order):
    for axis, bit in order:
        size, dim = lax.axis_size(axis), AXES.index(axis)
        mine = lax.rem(lax.axis_index(axis) // bit, 2)
        shape = blocks.shape
        pairs = blocks.reshape(shape[:dim] + (shape[dim] // 2, 2) + shape[dim + 1 :])
        keep = lax.dynamic_index_in_dim(pairs, mine, dim + 1, keepdims=False)
        give = lax.dynamic_index_in_dim(pairs, 1 - mine, dim + 1, keepdims=False)
        got = lax.ppermute(
            give.astype(jnp.bfloat16), axis, [(i, i ^ bit) for i in range(size)]
        )
        blocks = keep + got.astype(jnp.float32)
    return blocks[0, 0]


def bits_of(axis):
    return [(axis, 1 << at) for at in range(lax.axis_size(axis).bit_length() - 1)]


def per_device(features, prototypes, crop_sample, crop_live):
    row_count, width = features.shape
    proto_devs = lax.axis_size("proto")
    sec_devs = lax.axis_size("sec")
    teach_devs = sec_devs // 4
    first_dev = sec_devs // 2 - teach_devs // 2
    sample_count = row_count * teach_devs
    cols = prototypes.shape[1] // sec_devs
    protos = prototypes.shape[1] * proto_devs
    chunk = math.gcd(cols, 2048)
    sec_index = lax.axis_index("sec")
    sec_array = sec_index.astype(jnp.int32).reshape(1)
    is_student = jnp.logical_or(sec_index < first_dev, sec_index >= first_dev + teach_devs)

    own_rows = unit_rows_of(features)
    sample = jnp.where(is_student, crop_sample, 0)
    digits = jnp.concatenate([sample // 128, sample % 128]).astype(jnp.bfloat16)
    extra = -(-digits.shape[0] // (32 * width)) * 32
    digits = jnp.pad(digits, (0, extra * width - digits.shape[0])).reshape(extra, width)
    packed = gather_rows(jnp.concatenate([own_rows, digits]), ITERS + 1)
    all_rows = packed[:, :row_count]
    all_digits = packed[:, row_count:].reshape(sec_devs, -1)[:, : 2 * row_count].astype(jnp.int32)
    all_samples = all_digits[:, :row_count] * 128 + all_digits[:, row_count:]

    def students_of(blocks):
        return jnp.concatenate([blocks[:first_dev], blocks[first_dev + teach_devs :]])

    stud_rows = students_of(all_rows).reshape(-1, width)
    stud_samples = students_of(all_samples).reshape(-1)
    teach_rows = all_rows[first_dev : first_dev + teach_devs].reshape(-1, width)

    expo_tab, chunk_tops = teacher_expo(sec_array, teach_rows, prototypes, cols, chunk)
    groups = stud_rows.reshape(ITERS, -1, width)
    found = []
    top_part = jnp.max(chunk_tops, axis=0)
    part, top, total, (row_top,) = student_mean(
        groups[0], prototypes, cols, chunk, fold(jnp.maximum), [top_part], 0
    )
    found.append((part, top, total))
    factor = jnp.exp2((chunk_tops - row_top) * (LOG2E / TEACH_TEMP))
    weight = jnp.ones_like(row_top)
    for turn in range(1, ITERS):
        row_part = sweep(factor, weight, expo_tab, protos, chunk)
        part, top, total, (row_total,) = student_mean(
            groups[turn], prototypes, cols, chunk, fold(jnp.add), [row_part], turn
        )
        found.append((part, top, total))
        weight = 1.0 / (sample_count * row_total)
    stud_part, stud_top, stud_total = [jnp.concatenate(pieces) for pieces in zip(*found)]
    target_part, target_total = target_mean(
        sec_array, factor, weight, expo_tab, prototypes, protos, chunk
    )
    pick = (stud_samples[:, None] == jnp.arange(sample_count)[None, :]).astype(jnp.bfloat16)
    chosen_part = jnp.dot(
        pick, target_part.astype(jnp.bfloat16), preferred_element_type=jnp.float32
    )
    cross_part = jnp.sum(stud_rows.astype(jnp.float32) * chosen_part, axis=1, keepdims=True)
    global_top, stud_total, target_total, cross = share(
        fold_softmax(-(-stud_top.size // 1024) * 8),
        [stud_top, stud_total, target_total, cross_part],
        ITERS,
    )
    shrink = jnp.exp2((stud_top - global_top) * (LOG2E / STUD_TEMP))
    chosen_total = jnp.sum(
        jnp.where(pick > 0, target_total.reshape(1, -1), 0.0), axis=1, keepdims=True
    )
    gap_part = stud_part * (shrink / stud_total) - chosen_part / chosen_total
    gap_part = gap_part.reshape(-1, row_count, width)
    blank = jnp.zeros((teach_devs, row_count, width), jnp.float32)
    blocks = jnp.concatenate([gap_part[:first_dev], blank, gap_part[first_dev:]])
    blocks = blocks.reshape(sec_devs, proto_devs, row_count // proto_devs, width)
    over_sec, over_proto = bits_of("sec"), bits_of("proto")
    one = halve(blocks[..., : width // 2], over_sec + over_proto)
    two = halve(
        blocks[..., width // 2 :], over_sec[:1] + over_proto[:1] + over_sec[1:] + over_proto[1:]
    )
    gap = jnp.concatenate([one, two], axis=1)

    loss = global_top / STUD_TEMP + jnp.log(stud_total) - cross / chosen_total / STUD_TEMP
    place = jnp.where(sec_index < first_dev, sec_index, sec_index - teach_devs)
    place = jnp.where(is_student, place, 0)
    own_loss = lax.dynamic_index_in_dim(loss.reshape(-1, row_count), place, 0, keepdims=False)
    live = crop_live.astype(jnp.float32) * is_student.astype(jnp.float32)
    crop_loss = jnp.where(live > 0, live * own_loss, 0.0)
    out_rows = row_count // proto_devs
    start = lax.axis_index("proto") * out_rows
    my_live = lax.dynamic_slice_in_dim(live, start, out_rows, 0)[:, None]
    embed_grad = jnp.where(my_live > 0, my_live * gap / STUD_TEMP, 0.0)
    return (crop_loss, embed_grad)


def solution(mesh):
    in_specs = (P("sec", None), P(None, "proto"), P("sec"), P("sec"))
    out_specs = (P("sec"), P(("sec", "proto"), None))
    return jax.shard_map(
        per_device, mesh=mesh, in_specs=in_specs, out_specs=out_specs, check_vma=False
    )
```
